32 devices in a mesh: clip: 8 (over z, x), patch: 4 (over y, core).
Axes of the slice: x: 2, y: 2, z: 4, core: 2. Of those that a mesh axis runs over, the one named last changes fastest.
Arguments:
- pixels: bfloat16 [128, 16, 64, 384], P(('clip', 'patch')), may hold values from -40 to 40
- destination: int32 [128, 1], P(('clip', 'patch')), may hold values from 0 to 7; in each aligned block of 4 rows (0 to 3, 4 to 7, ...) at most 2 rows name the same one
- embed_weight: bfloat16 [384, 128], replicated, may hold values from -0.3125 to 0.3125
- embed_gain: float32 [128], replicated, may hold values from 0.5 to 2
- mixing_weight: bfloat16 [9, 384, 256], replicated, may hold values from -0.109375 to 0.109375
- mixing_gain: float32 [256], replicated, may hold values from 0.5 to 2
- project_weight: bfloat16 [256, 512], replicated, may hold values from -0.375 to 0.375
- project_gain: float32 [512], replicated, may hold values from 0.25 to 1.75
Outputs:
- latents: bfloat16 [512, 8, 64, 512], P('clip', None, 'patch')
The draws below stay inside these ranges and needn't reach their ends.
Inputs may be any that keep to these rules, and one draw needn't show every extreme that they name: `destination`: among the 4 clips of one owner device (aligned blocks of 4 rows) no tokenizer index occurs more than 2 times, and some index occurs exactly 2 times in some blocks.
All inputs are finite; a program needn't handle non-finite values.
Results may differ from the reference program's by a relative error of at most 0.0059.
Values may be sent and summed in bfloat16 or wider, within the bound.
No kernel may reach another device: no remote copies, remote signals or barrier semaphores. Data moves between devices by JAX's collectives and lax.ppermute only.
A program may use at most 128 MiB of HBM per device.

```python
import math
import jax
import jax.numpy as jnp
import numpy as np
from jax import lax

GRID = 8
TUBE = 384
C1 = 128
C2 = 256
C3 = 512
GROUPS = 32
CAP = 2
LT1 = 16
LT2 = 8
POS = 64
OWN = 4
CLIPS = 128
SLOTS = 512
N_CLIP = 8
N_PATCH = 4


def draw_pixels(key, part):
    first, second, third = jax.random.split(key, 3)
    shape = (CLIPS, LT1, POS, TUBE)
    row_scale = jnp.exp(jax.random.uniform(second, (CLIPS, LT1, POS, 1), jnp.float32, 0.0, math.log(10.0)))
    col_scale = jnp.exp(jax.random.uniform(third, (CLIPS, 1, 1, TUBE), jnp.float32, 0.0, math.log(10.0)))
    base = jnp.clip(jax.random.normal(first, shape, jnp.float32), -4.0, 4.0)
    return (0.1 * base * row_scale * col_scale).astype(jnp.bfloat16)


def assign_block(rng, own, number, rows, number_of, top, most, lean):
    sequence = jax.random.permutation(rng, number_of)
    packed, common = portions_of(number_of, rows * top, most, lean, True), portions_of(number_of, rows * top, most, lean, False)
    places = jnp.arange(number_of)

    def named(lengths, turn):
        used = int((lengths > 0).sum())
        fixed = max(1, used // 4)
        passed = fixed + (places - fixed + turn * (used - fixed)) % max(1, number_of - fixed)
        return jnp.zeros((number_of,), jnp.int32).at[sequence[jnp.where(places < fixed, places, passed)]].set(jnp.asarray(lengths, jnp.int32))

    lengths = jnp.where(number % 4 == 0, named(packed, number // 4), named(common, number - number // 4 - 1))
    mixed = jax.random.permutation(jax.random.fold_in(own, 3), number_of)
    source_of, receiver = mixed[0:number_of // 2 * 2:2], mixed[1:number_of // 2 * 2:2]
    slack = jnp.minimum(lengths[source_of] - 1, most - lengths[receiver]) // 2
    slack = jnp.where((source_of == sequence[0]) | (receiver == sequence[0]) | (lengths[receiver] == 0), 0, jnp.maximum(slack, 0))
    passed = jax.random.randint(jax.random.fold_in(own, 4), (number_of // 2,), 0, 1 << 20) % (slack + 1)
    lengths = lengths.at[source_of].add(-passed).at[receiver].add(passed)
    labels = jnp.searchsorted(jnp.cumsum(lengths), jnp.arange(rows * top), side="right").astype(jnp.int32)
    listing = labels.reshape(top, rows).T
    listing = listing[jax.random.permutation(jax.random.fold_in(own, 1), rows)]
    turn = jax.random.randint(jax.random.fold_in(own, 2), (rows, 1), 0, top)
    return jnp.take_along_axis(listing, (jnp.arange(top)[None, :] + turn) % top, axis=1)


def portions_of(amount, total, most, slope, full):
    weights = [(1 << 20) // math.isqrt(rank ** slope) + 1 for rank in range(1, amount + 1)]
    largest = most if full else min(most, max(-(-total // amount), total * weights[0] // sum(weights)))
    least = 1 if total - largest >= amount - 1 else 0
    counts, spare = [largest] + [least] * (amount - 1), total - largest - least * (amount - 1)
    while spare > 0:
        free = [i for i in range(1, amount) if counts[i] < largest] or [i for i in range(1, amount) if counts[i] < most]
        mass, budget = sum([weights[i] for i in free]), spare
        for i in free:
            extra = min(most - counts[i], max(1, budget * weights[i] // mass), spare)
            counts[i] = counts[i] + extra
            spare = spare - extra
    return np.array(counts)


def gaussian(stream_key, dims, deviation, limit, held_as=jnp.bfloat16):
    return jnp.clip(deviation * jax.random.normal(stream_key, dims, jnp.float32), -limit, limit).astype(held_as)


def setup_inputs(seed: int = 0) -> dict:
    streams_of = jax.random.split(jax.random.key(seed), 9)
    pixels = draw_pixels(jax.random.fold_in(streams_of[8], 71), 0)
    destination_keys = jax.random.split(jax.random.fold_in(streams_of[1], 1), CLIPS // OWN)
    destination_turns = jax.random.permutation(jax.random.fold_in(streams_of[1], 3), CLIPS // OWN)
    destination = jax.vmap(lambda own, number: assign_block(jax.random.fold_in(streams_of[1], 2), own, number, OWN, N_CLIP, 1, CAP, 2))(destination_keys, destination_turns).reshape((CLIPS, 1))
    embed_weight = gaussian(streams_of[2], (TUBE, C1), TUBE ** -0.5, 0.3125)
    embed_gain = jnp.clip(jnp.exp(jax.random.uniform(streams_of[3], (C1,), jnp.float32, math.log(0.5), math.log(2.0))), 0.5, 2.0)
    mixing_weight = gaussian(streams_of[4], (9, 3 * C1, C2), (27 * C1) ** -0.5, 0.109375)
    mixing_gain = jnp.clip(jnp.exp(jax.random.uniform(streams_of[5], (C2,), jnp.float32, math.log(0.5), math.log(2.0))), 0.5, 2.0)
    project_weight = gaussian(streams_of[6], (C2, C3), C2 ** -0.5, 0.375)
    project_gain = jnp.clip(1.0 + 0.15 * jax.random.normal(streams_of[7], (C3,), jnp.float32), 0.25, 1.75)
    return {"pixels": pixels, "destination": destination, "embed_weight": embed_weight, "embed_gain": embed_gain, "mixing_weight": mixing_weight, "mixing_gain": mixing_gain, "project_weight": project_weight, "project_gain": project_gain}


def group_norm(values, scales):
    number, frames, places, channels = values.shape
    grouped = values.reshape(number, frames, places, GROUPS, channels // GROUPS)
    average = lax.optimization_barrier(jnp.mean(grouped, axis=(1, 2, 4), keepdims=True))
    centred = grouped - average
    spread = lax.optimization_barrier(jnp.mean(centred * centred, axis=(1, 2, 4), keepdims=True))
    return (centred * lax.rsqrt(spread + 1e-05)).reshape(number, frames, places, channels) * scales

def encode(tubes, embed_weight, embed_gain, mixing_weight, mixing_gain, project_weight, project_gain):
    number, frames, places, breadth = tubes.shape
    embedded = jnp.dot(tubes.reshape(-1, breadth), embed_weight, preferred_element_type=jnp.float32)
    embedded = embedded.reshape(number, frames, places, -1)
    first_act = jax.nn.silu(group_norm(embedded, embed_gain)).astype(jnp.bfloat16)
    channels = first_act.shape[-1]
    padded = jnp.concatenate([jnp.zeros((number, 1, places, channels), jnp.bfloat16), first_act], axis=1)
    latent_frames = frames // 2
    stacked = jnp.concatenate([padded[:, time_tap:time_tap + 2 * latent_frames - 1:2] for time_tap in range(3)], axis=-1)
    stacked = stacked.reshape(number, latent_frames, GRID, GRID, 3 * channels)
    stacked = jnp.pad(stacked, ((0, 0), (0, 0), (1, 1), (1, 1), (0, 0)))
    summed = jnp.zeros((number * latent_frames * places, mixing_weight.shape[-1]), jnp.float32)
    for row_tap in range(3):
        for col_tap in range(3):
            window = stacked[:, :, row_tap:row_tap + GRID, col_tap:col_tap + GRID].reshape(-1, 3 * channels)
            summed = summed + jnp.dot(window, mixing_weight[row_tap * 3 + col_tap], preferred_element_type=jnp.float32)
    second = summed.reshape(number, latent_frames, places, -1)
    second_act = jax.nn.silu(group_norm(second, mixing_gain)).astype(jnp.bfloat16)
    projected = jnp.dot(second_act.reshape(-1, second_act.shape[-1]), project_weight, preferred_element_type=jnp.float32)
    projected = projected.reshape(number, latent_frames, places, -1)
    return group_norm(projected, project_gain).astype(jnp.bfloat16)

def reference(pixels, destination, embed_weight, embed_gain, mixing_weight, mixing_gain, project_weight, project_gain):
    owners = N_CLIP * N_PATCH
    targets = destination.reshape(owners, OWN)
    same = targets[:, :, None] == targets[:, None, :]
    order = jnp.arange(OWN, dtype=jnp.int32)
    earlier = order[:, None] > order[None, :]
    ranks = lax.optimization_barrier(jnp.sum((same & earlier[None]).astype(jnp.int32), axis=2)).astype(jnp.int32)
    owner_ids = jnp.arange(owners, dtype=jnp.int32)[:, None]
    slots = targets * (N_PATCH * N_CLIP * CAP) + owner_ids % N_PATCH * (N_CLIP * CAP) + owner_ids // N_PATCH * CAP + ranks

    def one_owner(block):
        return encode(block, embed_weight, embed_gain, mixing_weight, mixing_gain, project_weight, project_gain)
    encoded = lax.map(one_owner, pixels.reshape(owners, OWN, LT1, POS, TUBE))
    latents = jnp.zeros((SLOTS, LT2, POS, C3), jnp.bfloat16)
    return latents.at[slots.reshape(-1)].set(encoded.reshape(-1, LT2, POS, C3))
```

```python
import functools

import jax
import jax.numpy as jnp
import ml_dtypes
import numpy as np
from jax import lax
from jax.experimental import pallas as pl
from jax.experimental.pallas import tpu as pltpu
from jax.sharding import PartitionSpec as P

GRID = 8
GROUPS = 32
CAP = 2
TILE = 16
PARTS = 3
CHUNKS = 2
NAMES = 2 * PARTS * GROUPS
F32, BF16 = jnp.float32, jnp.bfloat16


def spread_table(latent, chunk):
    table = np.zeros((3, chunk, latent, 2 * latent, chunk), np.float32)
    places = np.arange(chunk)
    for tap in range(3):
        for step in range(latent):
            if 2 * step - 1 + tap >= 0:
                table[tap, places, step, 2 * step - 1 + tap, places] = 1
    return table.reshape(3 * chunk * latent, 2 * latent * chunk)


def swap_table(latent, share):
    table = np.zeros((latent, share, share, latent), np.float32)
    for step in range(latent):
        table[step, np.arange(share), np.arange(share), step] = 1
    return table.reshape(latent * share, latent * share)


def fold_table(channels, lanes):
    width = channels // GROUPS
    group = np.arange(lanes) // width
    return (group[:, None] == group[None, :]).astype(np.float32) / width


def pick_table(channels):
    table = np.zeros((channels, 256), np.float32)
    lanes = np.arange(NAMES)
    table[lanes % GROUPS * (channels // GROUPS), lanes] = 1
    return table


def place_table(channels):
    table = np.zeros((256, 2, channels), np.float32)
    lanes = np.arange(NAMES)
    of_group = lanes[:, None] % GROUPS == np.arange(channels)[None, :] // (channels // GROUPS)
    for which in range(2):
        mine = lanes // (PARTS * GROUPS) == which
        table[:NAMES, which] = of_group & mine[:, None]
    return table.reshape(256, 2 * channels)


def stacked(tables):
    rows = [np.pad(t, ((0, 0), (0, 256 - t.shape[1]))) for t in tables]
    starts = np.cumsum([0] + [r.shape[0] for r in rows])
    return np.concatenate(rows).astype(ml_dtypes.bfloat16), [int(s) for s in starts]


def split(row):
    parts = []
    for _ in range(PARTS):
        head = row.astype(BF16)
        parts.append(head)
        row = row - head.astype(F32)
    return parts


def fold(row, table):
    lanes = table.shape[0]
    halves = row.shape[1] // lanes
    parts = [part.astype(F32) for part in split(row)]
    rows = [part[:, h * lanes : (h + 1) * lanes] for h in range(halves) for part in parts]
    rows.append(jnp.zeros((TILE - len(rows), lanes), F32))
    out = jnp.dot(jnp.concatenate(rows, axis=0).astype(BF16), table, preferred_element_type=F32)
    sums = [jnp.sum(out[PARTS * h : PARTS * (h + 1)], axis=0, keepdims=True) for h in range(halves)]
    return jnp.concatenate(sums, axis=1)


def centre(values, table):
    share = 1.0 / values.shape[0]
    average = fold(jnp.sum(values, axis=0, keepdims=True) * share, table)
    centred = values - average
    power = fold(jnp.sum(centred * centred, axis=0, keepdims=True) * share, table)
    return average, centred, lax.rsqrt(power + 1e-05)


def silu(v):
    half = 0.5 * v
    return half + half * jnp.tanh(half)


def encode_kernel(named, x, w1, g1, w2, g2, w3, tables, *rest, starts, shares, owned):
    sends, (wide, act) = rest[:shares], rest[shares:]
    _, frames, places, breadth = x.shape
    latent = frames // 2
    c1, c2 = w1.shape[1], w2.shape[2]
    line = GRID * latent
    share = places * latent // shares
    spread = tables[starts[0] : starts[1]]
    swap = tables[starts[1] : starts[2], 0:share]
    fold1 = tables[starts[2] : starts[3], 0:c1]
    fold2 = tables[starts[3] : starts[4], 0:c2]
    fold3 = tables[starts[4] : starts[5]]
    pick = tables[starts[5] : starts[6]]
    chunk = spread.shape[1] // frames
    clip = pl.program_id(0)
    clips = pl.num_programs(0)

    @pl.when(clip == 0)
    def _():
        wide[0:line, :] = jnp.zeros((line, wide.shape[1]), BF16)
        wide[(GRID + 1) * line :, :] = jnp.zeros((line, wide.shape[1]), BF16)

    first = jnp.dot(x[0].reshape(frames * places, breadth), w1[...], preferred_element_type=F32)
    _, centred, scale = centre(first, fold1)
    act1 = silu(centred * (scale * g1[...])).astype(BF16).reshape(frames, places, c1)
    for q in range(places // chunk):
        block = act1[:, q * chunk : (q + 1) * chunk].reshape(frames * chunk, c1)
        taps = jnp.dot(spread, block, preferred_element_type=F32)
        taps = taps.reshape(3, chunk // GRID, GRID, latent, c1)
        edge = jnp.zeros((chunk // GRID, 1, latent, c1), F32)
        at = line + q * chunk * latent
        for a in range(3):
            for j in range(3):
                tap = taps[a]
                if j == 0:
                    tap = jnp.concatenate([edge, tap[:, : GRID - 1]], axis=1)
                if j == 2:
                    tap = jnp.concatenate([tap[:, 1:], edge], axis=1)
                tap = tap.reshape(chunk * latent, c1).astype(BF16)
                wide[at : at + chunk * latent, (3 * j + a) * c1 : (3 * j + a + 1) * c1] = tap
    rows = places * latent
    second = jnp.dot(wide[0:rows], w2[0], preferred_element_type=F32)
    for i in (1, 2):
        second += jnp.dot(wide[i * line : i * line + rows], w2[i], preferred_element_type=F32)
    _, centred, scale = centre(second, fold2)
    act2 = silu(centred * (scale * g2[...])).astype(BF16)
    act[...] = act2
    third = jnp.dot(act2, w3[...], preferred_element_type=F32)
    average, _, scale = centre(third, fold3)
    parts = [part.astype(F32) for part in split(average) + split(scale)]
    parts.append(jnp.zeros((TILE - len(parts), third.shape[1]), F32))
    picked = jnp.dot(jnp.concatenate(parts, axis=0).astype(BF16), pick, preferred_element_type=F32)
    lane = lax.broadcasted_iota(jnp.int32, (1, 256), 1)
    note = jnp.zeros((1, 256), F32)
    for k in range(2 * PARTS):
        note = jnp.where(lane // GROUPS == k, picked[k : k + 1], note)
    for k in range(owned):
        note = jnp.where(lane == NAMES + k, named[1 + k].astype(F32), note)
    row = lax.broadcasted_iota(jnp.int32, (TILE, 256), 0)
    body = sends[0].shape[0] - TILE
    for j in range(shares):
        q = named[0] ^ j
        part = act[pl.ds(pl.multiple_of(q * share, share), share), :]
        part = jnp.dot(swap, part, preferred_element_type=F32).astype(BF16)
        sends[j][pl.ds(pl.multiple_of(clip * share, share), share), :] = part

        @pl.when(clip == 0)
        def _():
            sends[j][body : body + TILE, :] = jnp.where(row == 0, note, 0.0).astype(BF16)

        @pl.when(clip > 0)
        def _():
            held = sends[j][body : body + TILE, :].astype(F32)
            sends[j][body : body + TILE, :] = jnp.where(row == clip, note, held).astype(BF16)


def encode(named, pixels, weights, start, count, shares):
    w1, g1, w2, g2, w3 = weights
    owned, frames, places, breadth = pixels.shape
    latent = frames // 2
    c1, c2, c3 = w1.shape[1], w2.shape[2], w3.shape[1]
    share = latent * places // shares
    tables, starts = stacked([
        spread_table(latent, 2 * GRID),
        swap_table(latent, places // shares),
        fold_table(c1, c1),
        fold_table(c2, c2),
        fold_table(c3, 256),
        pick_table(c3),
    ])
    operands = [w1, g1.reshape(1, c1), w2.reshape(3, 3 * w2.shape[1], c2), g2.reshape(1, c2), w3]
    operands.append(jnp.asarray(tables))
    whole = [pl.BlockSpec(o.shape, lambda i, s, n=o.ndim: (0,) * n) for o in operands]
    body = count * share + TILE
    flops = 2 * frames * places * breadth * c1 + 2 * latent * places * (27 * c1 * c2 + c2 * c3)
    return pl.pallas_call(
        functools.partial(encode_kernel, starts=starts, shares=shares, owned=owned),
        grid_spec=pltpu.PrefetchScalarGridSpec(
            num_scalar_prefetch=1,
            grid=(count,),
            in_specs=[pl.BlockSpec((1, frames, places, breadth), lambda i, s: (start + i, 0, 0, 0))] + whole,
            out_specs=[pl.BlockSpec((body, c2), lambda i, s: (0, 0))] * shares,
            scratch_shapes=[
                pltpu.VMEM(((GRID + 2) * GRID * latent, 9 * c1), BF16),
                pltpu.VMEM((places * latent, c2), BF16),
            ],
        ),
        out_shape=[jax.ShapeDtypeStruct((body, c2), BF16)] * shares,
        compiler_params=pltpu.CompilerParams(vmem_limit_bytes=40 * 1024 * 1024),
        cost_estimate=pl.CostEstimate(
            flops=count * flops, bytes_accessed=count * frames * places * breadth * 2, transcendentals=0
        ),
        name="encode",
    )(named, pixels, *operands)


def pack_kernel(table, sel, *rest, shares, per, share):
    half = sel.shape[0]
    held = [rest[g * shares : (g + 1) * shares] for g in range(CHUNKS)]
    outs = rest[CHUNKS * shares : CHUNKS * shares + half]
    notes, ready, note_sem, block_sem, out_sem = rest[CHUNKS * shares + half :]
    waits = []
    for g in range(CHUNKS):
        for j in range(shares):
            k = g * shares + j
            copy = pltpu.make_async_copy(
                held[g][j].at[pl.ds(per * share, TILE)], notes.at[pl.ds(k * TILE, TILE)], note_sem.at[k]
            )
            copy.start()
            waits.append(copy)
    blocks = []
    for s in range(half):
        for j in range(shares):
            for r in range(CAP):
                k = (s * shares + j) * CAP + r
                clip = table[1 + k]
                to = pl.multiple_of(((table[0] ^ j) * CAP + r) * share, share)
                for g in range(CHUNKS):

                    @pl.when(clip // per == g)
                    def _():
                        at = pl.multiple_of((clip - g * per) * share, share)
                        pltpu.make_async_copy(
                            held[g][j].at[pl.ds(at, share)], outs[s].at[pl.ds(to, share)], block_sem.at[k]
                        ).start()

                blocks.append(
                    pltpu.make_async_copy(
                        held[0][j].at[pl.ds(0, share)], outs[s].at[pl.ds(to, share)], block_sem.at[k]
                    )
                )
    for copy in waits:
        copy.wait()
    tail = shares * CAP * share
    for s in range(half):
        ready[s] = jnp.dot(sel[s], notes[...], preferred_element_type=F32).astype(BF16)
        copy = pltpu.make_async_copy(ready.at[s], outs[s].at[pl.ds(tail, TILE)], out_sem.at[s])
        copy.start()
        blocks.append(copy)
    for copy in blocks:
        copy.wait()


def pack(me, node, half, held, per, share):
    shares = len(held[0])
    body, channels = held[0][0].shape
    owned = CHUNKS * per
    names = jnp.stack([h[body - TILE, NAMES : NAMES + owned] for h in held[0]]).astype(jnp.int32)
    order = jnp.arange(owned, dtype=jnp.int32)
    same = names[:, :, None] == names[:, None, :]
    ranks = jnp.sum((same & (order[:, None] > order[None, :])).astype(jnp.int32), axis=2)
    tokenizer = node ^ jnp.arange(half, dtype=jnp.int32)
    hit = (names[None, :, None, :] == tokenizer[:, None, None, None]) & (
        ranks[None, :, None, :] == jnp.arange(CAP, dtype=jnp.int32)[None, None, :, None]
    )
    clip = jnp.sum(jnp.where(hit, order, 0), axis=3)
    table = jnp.concatenate([me.reshape(1), clip.reshape(-1)]).astype(jnp.int32)
    owner = jnp.arange(shares, dtype=jnp.int32)
    is_owner = owner[:, None] == (me ^ owner)[None, :]
    sel = hit[:, None] & is_owner[None, :, :, None, None]
    sel = sel.transpose(0, 1, 3, 2, 4).reshape(half, shares * CAP, shares, CHUNKS, per)
    sel = sel.transpose(0, 1, 3, 2, 4)
    sel = jnp.pad(sel, ((0, 0), (0, TILE - shares * CAP), (0, 0), (0, 0), (0, TILE - per)))
    sel = sel.reshape(half, TILE, CHUNKS * shares * TILE).astype(BF16)
    out_rows = shares * CAP * share + TILE
    anywhere = pl.BlockSpec(memory_space=pl.ANY)
    copies = half * shares * CAP
    return pl.pallas_call(
        functools.partial(pack_kernel, shares=shares, per=per, share=share),
        grid_spec=pltpu.PrefetchScalarGridSpec(
            num_scalar_prefetch=1,
            grid=(1,),
            in_specs=[pl.BlockSpec(sel.shape, lambda i, s: (0, 0, 0))] + [anywhere] * (CHUNKS * shares),
            out_specs=[anywhere] * half,
            scratch_shapes=[
                pltpu.VMEM((CHUNKS * shares * TILE, channels), BF16),
                pltpu.VMEM((half, TILE, channels), BF16),
                pltpu.SemaphoreType.DMA((CHUNKS * shares,)),
                pltpu.SemaphoreType.DMA((copies,)),
                pltpu.SemaphoreType.DMA((half,)),
            ],
        ),
        out_shape=[jax.ShapeDtypeStruct((out_rows, channels), BF16)] * half,
        compiler_params=pltpu.CompilerParams(vmem_limit_bytes=8 * 1024 * 1024),
        cost_estimate=pl.CostEstimate(flops=0, bytes_accessed=4 * copies * share * channels, transcendentals=0),
        name="pack",
    )(table, sel, *[h for chunk in held for h in chunk])


def finish_kernel(columns, w3, g3, place, *rest, count):
    taken, noted = rest[:count], rest[count : 2 * count]
    out, (mean, gain) = rest[-3], rest[-2:]
    k, p = pl.program_id(0), pl.program_id(1)
    c3 = w3.shape[1]
    _, _, cap, latent, share, _ = out.shape
    rows = latent * share
    for i in range(count):

        @pl.when(k == i)
        def _():
            @pl.when(p == 0)
            def _():
                wide = jnp.dot(noted[i][...], place[...], preferred_element_type=F32)
                mean[...] = wide[:, :c3]
                gain[...] = wide[:, c3:] * g3[...]

            third = jnp.dot(taken[i][...], w3[...], preferred_element_type=F32)
            for r in range(cap):
                at = pl.ds(p * cap + r, 1)
                token = (third[r * rows : (r + 1) * rows] - mean[at, :]) * gain[at, :]
                out[0, 0, r] = token.reshape(latent, share, c3).astype(BF16)


def finish(columns, arrays, w3, g3, shape, before=None):
    count = len(arrays)
    shares, _, cap, latent, share, c3 = shape
    rows = latent * share
    c2 = w3.shape[0]
    place = jnp.asarray(place_table(c3).astype(ml_dtypes.bfloat16))

    def block(i):
        return lambda k, p, s: (jnp.where(k == i, p, jnp.where(k < i, 0, shares - 1)), 0)

    last = shares * cap * rows // TILE
    specs = [pl.BlockSpec(o.shape, lambda k, p, s: (0, 0)) for o in (w3, g3, place)]
    specs += [pl.BlockSpec((cap * rows, c2), block(i)) for i in range(count)]
    specs += [pl.BlockSpec((TILE, c2), lambda k, p, s: (last, 0)) for i in range(count)]
    operands = [w3, g3, place, *arrays, *arrays]
    aliases = {}
    if before is not None:
        specs.append(pl.BlockSpec(memory_space=pl.ANY))
        aliases = {1 + len(operands): 0}
        operands.append(before)
    return pl.pallas_call(
        functools.partial(finish_kernel, count=count),
        grid_spec=pltpu.PrefetchScalarGridSpec(
            num_scalar_prefetch=1,
            grid=(count, shares),
            in_specs=specs,
            out_specs=pl.BlockSpec((1, 1, cap, latent, share, c3), lambda k, p, s: (p, s[k], 0, 0, 0, 0)),
            scratch_shapes=[pltpu.VMEM((TILE, c3), F32), pltpu.VMEM((TILE, c3), F32)],
        ),
        out_shape=jax.ShapeDtypeStruct(shape, BF16),
        input_output_aliases=aliases,
        compiler_params=pltpu.CompilerParams(vmem_limit_bytes=24 * 1024 * 1024),
        cost_estimate=pl.CostEstimate(
            flops=2 * count * shares * cap * rows * c2 * c3,
            bytes_accessed=count * shares * cap * rows * (c2 + c3) * 2,
            transcendentals=0,
        ),
        name="finish",
    )(columns, *operands)


def on_device(pixels, destination, embed_weight, embed_gain, mixing_weight, mixing_gain, project_weight, project_gain):
    nodes, shares = lax.axis_size("clip"), lax.axis_size("patch")
    node, me = lax.axis_index("clip").astype(jnp.int32), lax.axis_index("patch").astype(jnp.int32)
    half = nodes // 2
    owned, frames, places, _ = pixels.shape
    latent, c3 = frames // 2, project_weight.shape[1]
    per = owned // CHUNKS
    share = latent * places // shares
    weights = (embed_weight, embed_gain, mixing_weight, mixing_gain, project_weight)
    named = jnp.concatenate([me.reshape(1), destination[:, 0].astype(jnp.int32)])

    def to_share(array, j):
        if j == 0:
            return array
        return lax.ppermute(array, "patch", [(p, p ^ j) for p in range(shares)])

    def to_node(array, s):
        if s == 0:
            return array
        return lax.ppermute(array, "clip", [(c, c ^ s) for c in range(nodes)])

    def across(array, j):
        pairs = [(c * shares + p, (c ^ half) * shares + (p ^ j)) for c in range(nodes) for p in range(shares)]
        return lax.ppermute(array, ("clip", "patch"), pairs)

    near, far = [], []
    for g in range(CHUNKS):
        sends = encode(named, pixels, weights, g * per, per, shares)
        far.append([across(sends[j], j) for j in range(shares)])
        near.append([to_share(sends[j], j) for j in range(shares)])
    own = pack(me, node, half, near, per, share)
    own = [to_node(own[s], s) for s in range(half)]
    other = pack(me, node, half, far, per, share)
    other = [to_node(other[s], s) for s in range(half)]

    w3, g3 = project_weight, project_gain.reshape(1, c3)
    shape = (shares, nodes, CAP, latent, places // shares, c3)
    early = jnp.stack([node ^ s for s in range(half)] + [node ^ half])
    late = jnp.stack([node ^ half ^ s for s in range(1, half)])
    latents = finish(early, own + other[:1], w3, g3, shape)
    latents = finish(late, other[1:], w3, g3, shape, latents)
    return latents.reshape(shares * nodes * CAP, latent, places // shares, c3)


def solution(mesh):
    return jax.shard_map(
        on_device,
        mesh=mesh,
        in_specs=(
            P(("clip", "patch"), None, None, None),
            P(("clip", "patch"), None),
            P(),
            P(),
            P(),
            P(),
            P(),
            P(),
        ),
        out_specs=P("clip", None, "patch", None),
        check_vma=False,
    )
```

```python
import functools

import jax
import jax.numpy as jnp
import ml_dtypes
import numpy as np
from jax import lax
from jax.experimental import pallas as pl
from jax.experimental.pallas import tpu as pltpu
from jax.sharding import PartitionSpec as P

GRID = 8
GROUPS = 32
CAP = 2
TILE = 16
PARTS = 3
BATCH = 2
NAMES = 2 * PARTS * GROUPS
F32, BF16 = jnp.float32, jnp.bfloat16


def spread_table(latent, chunk):
    table = np.zeros((3, chunk, latent, 2 * latent, chunk), np.float32)
    places = np.arange(chunk)
    for tap in range(3):
        for step in range(latent):
            if 2 * step - 1 + tap >= 0:
                table[tap, places, step, 2 * step - 1 + tap, places] = 1
    return table.reshape(3 * chunk * latent, 2 * latent * chunk)


def swap_table(latent, share):
    table = np.zeros((latent, share, share, latent), np.float32)
    for step in range(latent):
        table[step, np.arange(share), np.arange(share), step] = 1
    return table.reshape(latent * share, latent * share)


def fold_table(channels, lanes):
    width = channels // GROUPS
    group = np.arange(lanes) // width
    return (group[:, None] == group[None, :]).astype(np.float32) / width


def pick_table(channels):
    table = np.zeros((channels, 256), np.float32)
    lanes = np.arange(NAMES)
    table[lanes % GROUPS * (channels // GROUPS), lanes] = 1
    return table


def place_table(channels):
    table = np.zeros((256, 2, channels), np.float32)
    lanes = np.arange(NAMES)
    of_group = lanes[:, None] % GROUPS == np.arange(channels)[None, :] // (channels // GROUPS)
    for which in range(2):
        mine = lanes // (PARTS * GROUPS) == which
        table[:NAMES, which] = of_group & mine[:, None]
    return table.reshape(256, 2 * channels)


def stacked(tables):
    rows = [np.pad(t, ((0, 0), (0, 256 - t.shape[1]))) for t in tables]
    starts = np.cumsum([0] + [r.shape[0] for r in rows])
    return np.concatenate(rows).astype(ml_dtypes.bfloat16), [int(s) for s in starts]


def split(row):
    parts = []
    for _ in range(PARTS):
        head = row.astype(BF16)
        parts.append(head.astype(F32))
        row = row - head.astype(F32)
    return parts


def fold(rows, table):
    lanes = table.shape[0]
    halves = rows[0].shape[1] // lanes
    stack = []
    for row in rows:
        parts = split(row)
        stack += [part[:, h * lanes : (h + 1) * lanes] for h in range(halves) for part in parts]
    spare = -len(stack) % TILE
    if spare:
        stack.append(jnp.zeros((spare, lanes), F32))
    out = jnp.dot(jnp.concatenate(stack, axis=0).astype(BF16), table, preferred_element_type=F32)
    sums = []
    for k in range(0, len(rows) * halves, halves):
        at = [PARTS * (k + h) for h in range(halves)]
        sums.append(jnp.concatenate([jnp.sum(out[i : i + PARTS], axis=0, keepdims=True) for i in at], axis=1))
    return sums


def centre(values, table):
    share = 1.0 / values[0].shape[0]
    averages = fold([jnp.sum(v, axis=0, keepdims=True) * share for v in values], table)
    centred = [v - average for v, average in zip(values, averages)]
    powers = fold([jnp.sum(v * v, axis=0, keepdims=True) * share for v in centred], table)
    return averages, centred, [lax.rsqrt(power + 1e-05) for power in powers]


def silu(v):
    half = 0.5 * v
    return half + half * jnp.tanh(half)


def encode_kernel(named, x, *rest, starts, shares, owned):
    given, rest = rest[:6], rest[6:]
    sends, rest = rest[:shares], rest[shares:]
    (w1, g1, w2, g2, w3, tables), (wide, act, sems) = rest[:6], rest[6:]
    me = lax.axis_index("patch").astype(jnp.int32)
    copies = [pltpu.make_async_copy(a, b, sems.at[i]) for i, (a, b) in enumerate(zip(given, rest[:6]))]
    step = pl.program_id(0)

    def arrive(*which):
        @pl.when(step == 0)
        def _():
            for i in which:
                copies[i].wait()

    batch, frames, places, breadth = x.shape
    latent = frames // 2
    c1, c2 = w1.shape[1], w2.shape[2]
    line = GRID * latent
    share = places * latent // shares
    chunk = 2 * GRID
    rows = places * latent

    @pl.when(step == 0)
    def _():
        for i in (0, 5, 1, 2, 3, 4):
            copies[i].start()
        for b in range(batch):
            wide[b, 0:line, :] = jnp.zeros((line, wide.shape[2]), BF16)
            wide[b, (GRID + 1) * line :, :] = jnp.zeros((line, wide.shape[2]), BF16)

    arrive(0, 5, 1)
    spread = tables[starts[0] : starts[1]]
    swap = tables[starts[1] : starts[2], 0:share]
    fold1 = tables[starts[2] : starts[3], 0:c1]
    fold2 = tables[starts[3] : starts[4], 0:c2]
    fold3 = tables[starts[4] : starts[5]]
    pick = tables[starts[5] : starts[6]]
    first = [
        jnp.dot(x[b].reshape(frames * places, breadth), w1[...], preferred_element_type=F32) for b in range(batch)
    ]
    _, centred, scales = centre(first, fold1)
    for b in range(batch):
        act1 = silu(centred[b] * (scales[b] * g1[...])).astype(BF16).reshape(frames, places, c1)
        for q in range(places // chunk):
            block = act1[:, q * chunk : (q + 1) * chunk].reshape(frames * chunk, c1)
            taps = jnp.dot(spread, block, preferred_element_type=F32)
            taps = taps.reshape(3, chunk // GRID, GRID, latent, c1)
            edge = jnp.zeros((chunk // GRID, 1, latent, c1), F32)
            at = line + q * chunk * latent
            for a in range(3):
                for j in range(3):
                    tap = taps[a]
                    if j == 0:
                        tap = jnp.concatenate([edge, tap[:, : GRID - 1]], axis=1)
                    if j == 2:
                        tap = jnp.concatenate([tap[:, 1:], edge], axis=1)
                    tap = tap.reshape(chunk * latent, c1).astype(BF16)
                    wide[b, at : at + chunk * latent, (3 * j + a) * c1 : (3 * j + a + 1) * c1] = tap
    arrive(2, 3, 4)
    second = []
    for b in range(batch):
        total = jnp.dot(wide[b, 0:rows], w2[0], preferred_element_type=F32)
        for i in (1, 2):
            total += jnp.dot(wide[b, i * line : i * line + rows], w2[i], preferred_element_type=F32)
        second.append(total)
    _, centred, scales = centre(second, fold2)
    third = []
    for b in range(batch):
        act2 = silu(centred[b] * (scales[b] * g2[...])).astype(BF16)
        act[b] = act2
        third.append(jnp.dot(act2, w3[...], preferred_element_type=F32))
    averages, _, scales = centre(third, fold3)
    lane = lax.broadcasted_iota(jnp.int32, (1, 256), 1)
    row = lax.broadcasted_iota(jnp.int32, (TILE, 256), 0)
    notes = jnp.zeros((TILE, 256), F32)
    for b in range(batch):
        parts = split(averages[b]) + split(scales[b])
        parts.append(jnp.zeros((TILE - len(parts), third[b].shape[1]), F32))
        picked = jnp.dot(jnp.concatenate(parts, axis=0).astype(BF16), pick, preferred_element_type=F32)
        note = jnp.zeros((1, 256), F32)
        for k in range(2 * PARTS):
            note = jnp.where(lane // GROUPS == k, picked[k : k + 1], note)
        for k in range(owned):
            note = jnp.where(lane == NAMES + k, named[k].astype(F32), note)
        notes = jnp.where(row == step * batch + b, note, notes)
    body = sends[0].shape[0] - TILE
    for j in range(shares):
        q = me ^ j
        for b in range(batch):
            part = act[b, pl.ds(pl.multiple_of(q * share, share), share), :]
            part = jnp.dot(swap, part, preferred_element_type=F32).astype(BF16)
            sends[j][pl.ds(pl.multiple_of((step * batch + b) * share, share), share), :] = part

        @pl.when(step == 0)
        def _():
            sends[j][body : body + TILE, :] = notes.astype(BF16)

        @pl.when(step > 0)
        def _():
            held = sends[j][body : body + TILE, :].astype(F32)
            sends[j][body : body + TILE, :] = (held + notes).astype(BF16)


def encode(named, pixels, weights, shares):
    w1, g1, w2, g2, w3 = weights
    owned, frames, places, breadth = pixels.shape
    latent = frames // 2
    c1, c2, c3 = w1.shape[1], w2.shape[2], w3.shape[1]
    share = latent * places // shares
    tables, starts = stacked([
        spread_table(latent, 2 * GRID),
        swap_table(latent, places // shares),
        fold_table(c1, c1),
        fold_table(c2, c2),
        fold_table(c3, 256),
        pick_table(c3),
    ])
    operands = [w1, g1.reshape(1, c1), w2.reshape(3, 3 * w2.shape[1], c2), g2.reshape(1, c2), w3]
    operands.append(jnp.asarray(tables))
    body = owned * share + TILE
    flops = 2 * frames * places * breadth * c1 + 2 * latent * places * (27 * c1 * c2 + c2 * c3)
    return pl.pallas_call(
        functools.partial(encode_kernel, starts=starts, shares=shares, owned=owned),
        grid_spec=pltpu.PrefetchScalarGridSpec(
            num_scalar_prefetch=1,
            grid=(owned // BATCH,),
            in_specs=[pl.BlockSpec((BATCH, frames, places, breadth), lambda i, s: (i, 0, 0, 0))]
            + [pl.BlockSpec(memory_space=pltpu.HBM)] * len(operands),
            out_specs=[pl.BlockSpec((body, c2), lambda i, s: (0, 0))] * shares,
            scratch_shapes=[pltpu.VMEM(o.shape, o.dtype) for o in operands]
            + [
                pltpu.VMEM((BATCH, (GRID + 2) * GRID * latent, 9 * c1), BF16),
                pltpu.VMEM((BATCH, places * latent, c2), BF16),
                pltpu.SemaphoreType.DMA((len(operands),)),
            ],
        ),
        out_shape=[jax.ShapeDtypeStruct((body, c2), BF16)] * shares,
        compiler_params=pltpu.CompilerParams(vmem_limit_bytes=60 * 1024 * 1024),
        cost_estimate=pl.CostEstimate(
            flops=owned * flops, bytes_accessed=owned * frames * places * breadth * 2, transcendentals=0
        ),
        name="encode",
    )(named, pixels, *operands)


def pack_kernel(ints, *rest, half, shares, owned, share):
    held, outs = rest[:shares], rest[shares : shares + half]
    notes, ready, note_sem, block_sem, out_sem = rest[shares + half :]
    me = lax.axis_index("patch").astype(jnp.int32)
    node = lax.axis_index("clip").astype(jnp.int32)
    body = owned * share
    waits = []
    for k in range(shares):
        copy = pltpu.make_async_copy(
            held[k].at[pl.ds(body, TILE)], notes.at[pl.ds(k * TILE, TILE)], note_sem.at[k]
        )
        copy.start()
        waits.append(copy)
    blocks, picks = [], []
    for s in range(half):
        for j in range(shares):
            seen = jnp.int32(0)
            found = [jnp.int32(0)] * CAP
            for i in range(owned):
                mine = ints[j * owned + i] == (node ^ s)
                for r in range(CAP):
                    found[r] = jnp.where(mine & (seen == r), i, found[r])
                seen = seen + mine.astype(jnp.int32)
            for r in range(CAP):
                k = (s * shares + j) * CAP + r
                clip = found[r]
                row = (me ^ j) * CAP + r
                to = pl.multiple_of(row * share, share)
                picks.append((jnp.where(seen > r, row, -1), clip))
                start = pl.multiple_of(clip * share, share)
                copy = pltpu.make_async_copy(
                    held[j].at[pl.ds(start, share)], outs[s].at[pl.ds(to, share)], block_sem.at[k]
                )
                copy.start()
                blocks.append(copy)
    for copy in waits:
        copy.wait()
    width = shares * TILE
    rows = lax.broadcasted_iota(jnp.int32, (TILE, width), 0)
    columns = lax.broadcasted_iota(jnp.int32, (TILE, width), 1)
    for s in range(half):
        sel = jnp.zeros((TILE, width), jnp.bool_)
        for j in range(shares):
            for r in range(CAP):
                row, clip = picks[(s * shares + j) * CAP + r]
                sel = sel | ((rows == row) & (columns == j * TILE + clip))
        sel = jnp.where(sel, 1.0, 0.0).astype(BF16)
        ready[s] = jnp.dot(sel, notes[...], preferred_element_type=F32).astype(BF16)
        copy = pltpu.make_async_copy(ready.at[s], outs[s].at[pl.ds(shares * CAP * share, TILE)], out_sem.at[s])
        copy.start()
        blocks.append(copy)
    for copy in blocks:
        copy.wait()


def pack(half, held, owned, share):
    shares, channels = len(held), held[0].shape[1]
    ints = jnp.concatenate([h[owned * share, NAMES : NAMES + owned] for h in held]).astype(jnp.int32)
    out_rows = shares * CAP * share + TILE
    anywhere = pl.BlockSpec(memory_space=pl.ANY)
    copies = half * shares * CAP
    return pl.pallas_call(
        functools.partial(pack_kernel, half=half, shares=shares, owned=owned, share=share),
        grid_spec=pltpu.PrefetchScalarGridSpec(
            num_scalar_prefetch=1,
            grid=(1,),
            in_specs=[anywhere] * shares,
            out_specs=[anywhere] * half,
            scratch_shapes=[
                pltpu.VMEM((shares * TILE, channels), BF16),
                pltpu.VMEM((half, TILE, channels), BF16),
                pltpu.SemaphoreType.DMA((shares,)),
                pltpu.SemaphoreType.DMA((copies,)),
                pltpu.SemaphoreType.DMA((half,)),
            ],
        ),
        out_shape=[jax.ShapeDtypeStruct((out_rows, channels), BF16)] * half,
        compiler_params=pltpu.CompilerParams(vmem_limit_bytes=8 * 1024 * 1024),
        cost_estimate=pl.CostEstimate(flops=0, bytes_accessed=2 * copies * share * channels, transcendentals=0),
        name="pack",
    )(ints, *held)


def finish_kernel(columns, w3, g3, place, *rest, count):
    taken, out = rest[:count], rest[-1]
    c3 = w3.shape[1]
    shares, _, cap, latent, share, _ = out.shape
    rows = latent * share
    for i in range(count):

        @pl.when(pl.program_id(0) == i)
        def _():
            wide = jnp.dot(taken[i][shares * cap * rows :, :], place[...], preferred_element_type=F32)
            mean, gain = wide[:, :c3], wide[:, c3:] * g3[...]
            for p in range(shares):
                block = taken[i][p * cap * rows : (p + 1) * cap * rows, :]
                third = jnp.dot(block, w3[...], preferred_element_type=F32)
                for r in range(cap):
                    at = p * cap + r
                    token = (third[r * rows : (r + 1) * rows] - mean[at : at + 1]) * gain[at : at + 1]
                    out[p, 0, r] = token.reshape(latent, share, c3).astype(BF16)


def finish(columns, arrays, w3, g3, shape, before=None):
    count = len(arrays)
    shares, _, cap, latent, share, c3 = shape
    rows = latent * share
    c2 = w3.shape[0]
    place = jnp.asarray(place_table(c3).astype(ml_dtypes.bfloat16))
    operands = [w3, g3, place, *arrays]
    specs = [pl.BlockSpec(o.shape, lambda k, s: (0, 0)) for o in operands]
    aliases = {}
    if before is not None:
        specs.append(pl.BlockSpec(memory_space=pl.ANY))
        aliases = {1 + len(operands): 0}
        operands.append(before)
    return pl.pallas_call(
        functools.partial(finish_kernel, count=count),
        grid_spec=pltpu.PrefetchScalarGridSpec(
            num_scalar_prefetch=1,
            grid=(count,),
            in_specs=specs,
            out_specs=pl.BlockSpec((shares, 1, cap, latent, share, c3), lambda k, s: (0, s[k], 0, 0, 0, 0)),
        ),
        out_shape=jax.ShapeDtypeStruct(shape, BF16),
        input_output_aliases=aliases,
        compiler_params=pltpu.CompilerParams(vmem_limit_bytes=24 * 1024 * 1024),
        cost_estimate=pl.CostEstimate(
            flops=2 * count * shares * cap * rows * c2 * c3,
            bytes_accessed=count * shares * cap * rows * (c2 + c3) * 2,
            transcendentals=0,
        ),
        name="finish",
    )(columns, *operands)


def on_device(pixels, destination, embed_weight, embed_gain, mixing_weight, mixing_gain, project_weight, project_gain):
    nodes, shares = lax.axis_size("clip"), lax.axis_size("patch")
    node = lax.axis_index("clip").astype(jnp.int32)
    half = nodes // 2
    owned, frames, places, _ = pixels.shape
    latent, c3 = frames // 2, project_weight.shape[1]
    share = latent * places // shares
    weights = (embed_weight, embed_gain, mixing_weight, mixing_gain, project_weight)
    named = destination.reshape(owned)

    def to_share(array, j):
        if j == 0:
            return array
        return lax.ppermute(array, "patch", [(p, p ^ j) for p in range(shares)])

    def to_node(array, s):
        if s == 0:
            return array
        return lax.ppermute(array, "clip", [(c, c ^ s) for c in range(nodes)])

    sends = encode(named, pixels, weights, shares)
    near = [to_share(sends[j], j) for j in range(shares)]
    far = [to_node(near[j], half) for j in range(shares)]
    own = pack(half, near, owned, share)
    own = [to_node(own[s], s) for s in range(half)]
    other = pack(half, far, owned, share)
    other = [to_node(other[s], s) for s in range(half)]

    w3, g3 = project_weight, project_gain.reshape(1, c3)
    shape = (shares, nodes, CAP, latent, places // shares, c3)
    early = jnp.stack([node ^ s for s in range(half)] + [node ^ half])
    latents = finish(early, own + other[:1], w3, g3, shape)
    for s in range(1, half):
        latents = finish((node ^ half ^ s).reshape(1), other[s : s + 1], w3, g3, shape, latents)
    return latents.reshape(shares * nodes * CAP, latent, places // shares, c3)


def solution(mesh):
    return jax.shard_map(
        on_device,
        mesh=mesh,
        in_specs=(
            P(("clip", "patch"), None, None, None),
            P(("clip", "patch"), None),
            P(),
            P(),
            P(),
            P(),
            P(),
            P(),
        ),
        out_specs=P("clip", None, "patch", None),
        check_vma=False,
    )
```

```python
import functools

import jax
import jax.numpy as jnp
import ml_dtypes
import numpy as np
from jax import lax
from jax.experimental import pallas as pl
from jax.experimental.pallas import tpu as pltpu
from jax.sharding import PartitionSpec as P

GRID = 8
GROUPS = 32
CAP = 2
TILE = 16
PARTS = 3
BATCH = 4
NAMES = 2 * PARTS * GROUPS
F32, BF16 = jnp.float32, jnp.bfloat16


def spread_table(latent, chunk):
    table = np.zeros((3, chunk, latent, 2 * latent, chunk), np.float32)
    places = np.arange(chunk)
    for tap in range(3):
        for step in range(latent):
            if 2 * step - 1 + tap >= 0:
                table[tap, places, step, 2 * step - 1 + tap, places] = 1
    return table.reshape(3 * chunk * latent, 2 * latent * chunk)


def swap_table(latent, share):
    table = np.zeros((latent, share, share, latent), np.float32)
    for step in range(latent):
        table[step, np.arange(share), np.arange(share), step] = 1
    return table.reshape(latent * share, latent * share)


def fold_table(channels, lanes):
    width = channels // GROUPS
    group = np.arange(lanes) // width
    return (group[:, None] == group[None, :]).astype(np.float32) / width


def pick_table(channels):
    table = np.zeros((channels, 256), np.float32)
    lanes = np.arange(NAMES)
    table[lanes % GROUPS * (channels // GROUPS), lanes] = 1
    return table


def place_table(channels):
    table = np.zeros((256, 2, channels), np.float32)
    lanes = np.arange(NAMES)
    of_group = lanes[:, None] % GROUPS == np.arange(channels)[None, :] // (channels // GROUPS)
    for which in range(2):
        mine = lanes // (PARTS * GROUPS) == which
        table[:NAMES, which] = of_group & mine[:, None]
    return table.reshape(256, 2 * channels)


def stacked(tables):
    rows = [np.pad(t, ((0, 0), (0, 256 - t.shape[1]))) for t in tables]
    starts = np.cumsum([0] + [r.shape[0] for r in rows])
    return np.concatenate(rows).astype(ml_dtypes.bfloat16), [int(s) for s in starts]


def split(row):
    parts = []
    for _ in range(PARTS):
        head = row.astype(BF16)
        parts.append(head.astype(F32))
        row = row - head.astype(F32)
    return parts


def fold(rows, table):
    lanes = table.shape[0]
    halves = rows[0].shape[1] // lanes
    stack = []
    for row in rows:
        parts = split(row)
        stack += [part[:, h * lanes : (h + 1) * lanes] for h in range(halves) for part in parts]
    spare = -len(stack) % TILE
    if spare:
        stack.append(jnp.zeros((spare, lanes), F32))
    out = jnp.dot(jnp.concatenate(stack, axis=0).astype(BF16), table, preferred_element_type=F32)
    sums = []
    for k in range(0, len(rows) * halves, halves):
        at = [PARTS * (k + h) for h in range(halves)]
        sums.append(jnp.concatenate([jnp.sum(out[i : i + PARTS], axis=0, keepdims=True) for i in at], axis=1))
    return sums


def centre(values, table):
    share = 1.0 / values[0].shape[0]
    averages = fold([jnp.sum(v, axis=0, keepdims=True) * share for v in values], table)
    centred = [v - average for v, average in zip(values, averages)]
    powers = fold([jnp.sum(v * v, axis=0, keepdims=True) * share for v in centred], table)
    return averages, centred, [lax.rsqrt(power + 1e-05) for power in powers]


def silu(v):
    half = 0.5 * v
    return half + half * jnp.tanh(half)


def encode_kernel(named, x, *rest, starts, shares, owned):
    given, rest = rest[:6], rest[6:]
    sends, rest = rest[:shares], rest[shares:]
    (w1, g1, w2, g2, w3, tables), (tubes, wide, act, sems, tube_sems) = rest[:6], rest[6:]
    me = lax.axis_index("patch").astype(jnp.int32)
    copies = [pltpu.make_async_copy(a, b, sems.at[i]) for i, (a, b) in enumerate(zip(given, rest[:6]))]
    step = pl.program_id(0)

    def arrive(*which):
        @pl.when(step == 0)
        def _():
            for i in which:
                copies[i].wait()

    batch, frames, places, breadth = tubes.shape
    loads = [pltpu.make_async_copy(x.at[step * batch + b], tubes.at[b], tube_sems.at[b]) for b in range(batch)]
    latent = frames // 2
    c1, c2 = w1.shape[1], w2.shape[2]
    line = GRID * latent
    share = places * latent // shares
    chunk = 2 * GRID
    rows = places * latent

    @pl.when(step == 0)
    def _():
        copies[0].start()

    loads[0].start()

    @pl.when(step == 0)
    def _():
        copies[5].start()
        copies[1].start()

    for load in loads[1:]:
        load.start()

    @pl.when(step == 0)
    def _():
        for i in (2, 3, 4):
            copies[i].start()
        for b in range(batch):
            wide[b, 0:line, :] = jnp.zeros((line, wide.shape[2]), BF16)
            wide[b, (GRID + 1) * line :, :] = jnp.zeros((line, wide.shape[2]), BF16)

    arrive(0, 5, 1)
    spread = tables[starts[0] : starts[1]]
    swap = tables[starts[1] : starts[2], 0:share]
    fold1 = tables[starts[2] : starts[3], 0:c1]
    fold2 = tables[starts[3] : starts[4], 0:c2]
    fold3 = tables[starts[4] : starts[5]]
    pick = tables[starts[5] : starts[6]]
    first = []
    for b in range(batch):
        loads[b].wait()
        first.append(jnp.dot(tubes[b].reshape(frames * places, breadth), w1[...], preferred_element_type=F32))
    _, centred, scales = centre(first, fold1)
    for b in range(batch):
        act1 = silu(centred[b] * (scales[b] * g1[...])).astype(BF16).reshape(frames, places, c1)
        for q in range(places // chunk):
            block = act1[:, q * chunk : (q + 1) * chunk].reshape(frames * chunk, c1)
            taps = jnp.dot(spread, block, preferred_element_type=F32)
            taps = taps.reshape(3, chunk // GRID, GRID, latent, c1)
            edge = jnp.zeros((chunk // GRID, 1, latent, c1), F32)
            at = line + q * chunk * latent
            for a in range(3):
                for j in range(3):
                    tap = taps[a]
                    if j == 0:
                        tap = jnp.concatenate([edge, tap[:, : GRID - 1]], axis=1)
                    if j == 2:
                        tap = jnp.concatenate([tap[:, 1:], edge], axis=1)
                    tap = tap.reshape(chunk * latent, c1).astype(BF16)
                    wide[b, at : at + chunk * latent, (3 * j + a) * c1 : (3 * j + a + 1) * c1] = tap
    arrive(2, 3, 4)
    second = []
    for b in range(batch):
        total = jnp.dot(wide[b, 0:rows], w2[0], preferred_element_type=F32)
        for i in (1, 2):
            total += jnp.dot(wide[b, i * line : i * line + rows], w2[i], preferred_element_type=F32)
        second.append(total)
    _, centred, scales = centre(second, fold2)
    third = []
    for b in range(batch):
        act2 = silu(centred[b] * (scales[b] * g2[...])).astype(BF16)
        act[b] = act2
        third.append(jnp.dot(act2, w3[...], preferred_element_type=F32))
    averages, _, scales = centre(third, fold3)
    lane = lax.broadcasted_iota(jnp.int32, (1, 256), 1)
    row = lax.broadcasted_iota(jnp.int32, (TILE, 256), 0)
    parts = [part for b in range(batch) for part in split(averages[b]) + split(scales[b])]
    parts.append(jnp.zeros((-len(parts) % TILE, third[0].shape[1]), F32))
    picked = jnp.dot(jnp.concatenate(parts, axis=0).astype(BF16), pick, preferred_element_type=F32)
    names = jnp.zeros((1, 256), F32)
    for k in range(owned):
        names = jnp.where(lane == NAMES + k, named[k].astype(F32), names)
    notes = jnp.zeros((TILE, 256), F32)
    for b in range(batch):
        note = names
        for k in range(2 * PARTS):
            at = 2 * PARTS * b + k
            note = jnp.where(lane // GROUPS == k, picked[at : at + 1], note)
        notes = jnp.where(row == step * batch + b, note, notes)
    body = sends[0].shape[0] - TILE
    for j in range(shares):
        q = me ^ j
        for b in range(batch):
            part = act[b, pl.ds(pl.multiple_of(q * share, share), share), :]
            part = jnp.dot(swap, part, preferred_element_type=F32).astype(BF16)
            sends[j][pl.ds(pl.multiple_of((step * batch + b) * share, share), share), :] = part

        @pl.when(step == 0)
        def _():
            sends[j][body : body + TILE, :] = notes.astype(BF16)

        @pl.when(step > 0)
        def _():
            held = sends[j][body : body + TILE, :].astype(F32)
            sends[j][body : body + TILE, :] = (held + notes).astype(BF16)


def encode(named, pixels, weights, shares):
    w1, g1, w2, g2, w3 = weights
    owned, frames, places, breadth = pixels.shape
    latent = frames // 2
    c1, c2, c3 = w1.shape[1], w2.shape[2], w3.shape[1]
    share = latent * places // shares
    tables, starts = stacked([
        spread_table(latent, 2 * GRID),
        swap_table(latent, places // shares),
        fold_table(c1, c1),
        fold_table(c2, c2),
        fold_table(c3, 256),
        pick_table(c3),
    ])
    operands = [w1, g1.reshape(1, c1), w2.reshape(3, 3 * w2.shape[1], c2), g2.reshape(1, c2), w3]
    operands.append(jnp.asarray(tables))
    body = owned * share + TILE
    flops = 2 * frames * places * breadth * c1 + 2 * latent * places * (27 * c1 * c2 + c2 * c3)
    return pl.pallas_call(
        functools.partial(encode_kernel, starts=starts, shares=shares, owned=owned),
        grid_spec=pltpu.PrefetchScalarGridSpec(
            num_scalar_prefetch=1,
            grid=(owned // BATCH,),
            in_specs=[pl.BlockSpec(memory_space=pltpu.HBM)] * (1 + len(operands)),
            out_specs=[pl.BlockSpec((body, c2), lambda i, s: (0, 0))] * shares,
            scratch_shapes=[pltpu.VMEM(o.shape, o.dtype) for o in operands]
            + [
                pltpu.VMEM((BATCH, frames, places, breadth), BF16),
                pltpu.VMEM((BATCH, (GRID + 2) * GRID * latent, 9 * c1), BF16),
                pltpu.VMEM((BATCH, places * latent, c2), BF16),
                pltpu.SemaphoreType.DMA((len(operands),)),
                pltpu.SemaphoreType.DMA((BATCH,)),
            ],
        ),
        out_shape=[jax.ShapeDtypeStruct((body, c2), BF16)] * shares,
        compiler_params=pltpu.CompilerParams(vmem_limit_bytes=60 * 1024 * 1024),
        cost_estimate=pl.CostEstimate(
            flops=owned * flops, bytes_accessed=owned * frames * places * breadth * 2, transcendentals=0
        ),
        name="encode",
    )(named, pixels, *operands)


def pack_kernel(ints, *rest, half, jobs, pick, owned, share):
    arrays = sum(len(job) for job in jobs)
    held, outs = rest[:arrays], rest[arrays : arrays + len(jobs) * half]
    notes, ready, note_sem, block_sem, out_sem = rest[arrays + len(jobs) * half :]
    me = lax.axis_index("patch").astype(jnp.int32)
    node = lax.axis_index("clip").astype(jnp.int32)
    owners = len(jobs[0])
    body = owned * share
    waits = []
    for k in range(owners):
        copy = pltpu.make_async_copy(held[k].at[pl.ds(body, TILE)], notes.at[pl.ds(k * TILE, TILE)], note_sem.at[k])
        copy.start()
        waits.append(copy)
    blocks, picks = [], []
    for s in range(half):
        for j in range(owners):
            seen = jnp.int32(0)
            found = [jnp.int32(0)] * CAP
            for i in range(owned):
                mine = ints[j * owned + i] == (node ^ s)
                for r in range(CAP):
                    found[r] = jnp.where(mine & (seen == r), i, found[r])
                seen = seen + mine.astype(jnp.int32)
            for r in range(CAP):
                clip = found[r]
                row = pick(me ^ jobs[0][j]) * CAP + r
                to = pl.multiple_of(row * share, share)
                start = pl.multiple_of(clip * share, share)
                picks.append((jnp.where(seen > r, row, -1), clip))
                for g in range(len(jobs)):
                    copy = pltpu.make_async_copy(
                        held[g * owners + j].at[pl.ds(start, share)],
                        outs[g * half + s].at[pl.ds(to, share)],
                        block_sem.at[len(blocks)],
                    )
                    copy.start()
                    blocks.append(copy)
    for copy in waits:
        copy.wait()
    width = owners * TILE
    rows = lax.broadcasted_iota(jnp.int32, (TILE, width), 0)
    columns = lax.broadcasted_iota(jnp.int32, (TILE, width), 1)
    for s in range(half):
        sel = jnp.zeros((TILE, width), jnp.bool_)
        for j in range(owners):
            for r in range(CAP):
                row, clip = picks[(s * owners + j) * CAP + r]
                sel = sel | ((rows == row) & (columns == j * TILE + clip))
        sel = jnp.where(sel, 1.0, 0.0).astype(BF16)
        ready[s] = jnp.dot(sel, notes[...], preferred_element_type=F32).astype(BF16)
    for s in range(half):
        for g in range(len(jobs)):
            k = g * half + s
            copy = pltpu.make_async_copy(
                ready.at[s], outs[k].at[pl.ds(owners * CAP * share, TILE)], out_sem.at[k]
            )
            copy.start()
            blocks.append(copy)
    for copy in blocks:
        copy.wait()


def pack(half, held, jobs, pick, owned, share):
    owners, channels = len(jobs[0]), held[0].shape[1]
    names = [h[owned * share, NAMES : NAMES + owned] for h in held[:owners]]
    ints = jnp.concatenate(names).astype(jnp.int32)
    out_rows = owners * CAP * share + TILE
    anywhere = pl.BlockSpec(memory_space=pl.ANY)
    count = len(jobs) * half
    copies = count * owners * CAP
    outs = pl.pallas_call(
        functools.partial(pack_kernel, half=half, jobs=jobs, pick=pick, owned=owned, share=share),
        grid_spec=pltpu.PrefetchScalarGridSpec(
            num_scalar_prefetch=1,
            grid=(1,),
            in_specs=[anywhere] * len(held),
            out_specs=[anywhere] * count,
            scratch_shapes=[
                pltpu.VMEM((owners * TILE, channels), BF16),
                pltpu.VMEM((half, TILE, channels), BF16),
                pltpu.SemaphoreType.DMA((owners,)),
                pltpu.SemaphoreType.DMA((copies,)),
                pltpu.SemaphoreType.DMA((count,)),
            ],
        ),
        out_shape=[jax.ShapeDtypeStruct((out_rows, channels), BF16)] * count,
        compiler_params=pltpu.CompilerParams(vmem_limit_bytes=8 * 1024 * 1024),
        cost_estimate=pl.CostEstimate(flops=0, bytes_accessed=2 * copies * share * channels, transcendentals=0),
        name="pack",
    )(ints, *held)
    return [outs[g * half : (g + 1) * half] for g in range(len(jobs))]


def finish_kernel(places, w3, g3, place, *rest, count):
    taken, out = rest[:count], rest[-1]
    c3 = w3.shape[1]
    lines, cores, _, cap, latent, share, _ = out.shape
    rows = latent * share
    owners = [(y, core) for y in range(lines) for core in range(cores)]
    for i in range(count):

        @pl.when(pl.program_id(0) == i)
        def _():
            wide = jnp.dot(taken[i][len(owners) * cap * rows :, :], place[...], preferred_element_type=F32)
            mean, gain = wide[:, :c3], wide[:, c3:] * g3[...]
            for p, (y, core) in enumerate(owners):
                block = taken[i][p * cap * rows : (p + 1) * cap * rows, :]
                third = jnp.dot(block, w3[...], preferred_element_type=F32)
                for r in range(cap):
                    at = p * cap + r
                    token = (third[r * rows : (r + 1) * rows] - mean[at : at + 1]) * gain[at : at + 1]
                    out[y, core, 0, r] = token.reshape(latent, share, c3).astype(BF16)


def finish(pieces, block, w3, g3, shape, before=None):
    count = len(pieces)
    cap, latent, share, c3 = shape[3:]
    rows = latent * share
    c2 = w3.shape[0]
    arrays = [piece[3] for piece in pieces]
    places = jnp.stack([jnp.asarray(piece[k], jnp.int32) for piece in pieces for k in range(3)])
    place = jnp.asarray(place_table(c3).astype(ml_dtypes.bfloat16))
    operands = [w3, g3, place, *arrays]
    specs = [pl.BlockSpec(o.shape, lambda k, s: (0, 0)) for o in operands]
    aliases = {}
    if before is not None:
        specs.append(pl.BlockSpec(memory_space=pl.ANY))
        aliases = {1 + len(operands): 0}
        operands.append(before)
    blocks = count * block[0] * block[1] * cap
    return pl.pallas_call(
        functools.partial(finish_kernel, count=count),
        grid_spec=pltpu.PrefetchScalarGridSpec(
            num_scalar_prefetch=1,
            grid=(count,),
            in_specs=specs,
            out_specs=pl.BlockSpec(
                (*block, 1, cap, latent, share, c3),
                lambda k, s: (s[3 * k], s[3 * k + 1], s[3 * k + 2], 0, 0, 0, 0),
            ),
        ),
        out_shape=jax.ShapeDtypeStruct(shape, BF16),
        input_output_aliases=aliases,
        compiler_params=pltpu.CompilerParams(vmem_limit_bytes=24 * 1024 * 1024),
        cost_estimate=pl.CostEstimate(
            flops=2 * blocks * rows * c2 * c3, bytes_accessed=blocks * rows * (c2 + c3) * 2, transcendentals=0
        ),
        name="finish",
    )(places, *operands)


def on_device(pixels, destination, embed_weight, embed_gain, mixing_weight, mixing_gain, project_weight, project_gain):
    nodes, shares = lax.axis_size("clip"), lax.axis_size("patch")
    node = lax.axis_index("clip").astype(jnp.int32)
    half = nodes // 2
    owned, frames, places, _ = pixels.shape
    latent, c3 = frames // 2, project_weight.shape[1]
    share = latent * places // shares
    weights = (embed_weight, embed_gain, mixing_weight, mixing_gain, project_weight)
    named = destination.reshape(owned)

    me = lax.axis_index("patch").astype(jnp.int32)
    lines = shares // 2
    w3, g3 = project_weight, project_gain.reshape(1, c3)
    shape = (lines, 2, nodes, CAP, latent, places // shares, c3)

    def send(array, s, j):
        if s == 0 and j == 0:
            return array
        pairs = [(c * shares + p, (c ^ s) * shares + (p ^ j)) for c in range(nodes) for p in range(shares)]
        return lax.ppermute(array, ("clip", "patch"), pairs)

    sends = encode(named, pixels, weights, shares)
    held = [sends[0::2], [send(array, 0, 1) for array in sends[1::2]]]
    pairs = [[held[0][k], held[1][k]] for k in range(lines)]
    own = pack(half, [a for pair in pairs for a in pair], [[0, 1]] * lines, lambda p: p % 2, owned, share)
    crossed = [send(held[0][k], half, 2 * k) for k in range(lines)]
    arrived = [[send(own[k][s], s, 2 * k) for s in range(half)] for k in range(lines)]
    pieces = [((me // 2) ^ k, 0, node ^ s, arrived[k][s]) for k in range(lines) for s in range(half)]
    def after(arrays, *earlier):
        return lax.optimization_barrier((*arrays, *earlier))[: len(arrays)]

    spread = [a for line in arrived[1:] for a in line]
    beyond = after(held[1], *crossed, *[a for line in own for a in line], arrived[0][1])
    beyond = [send(beyond[k], half, 2 * k) for k in range(lines)]
    early, late = [], []
    for b, far in enumerate((crossed, beyond)):
        if b:
            far = after(far, *spread, *arrived[0])
        (other,) = pack(half, list(far), [[2 * k + b for k in range(lines)]], lambda p: p // 2, owned, share)
        seconds = [send(other[s], s, 0) for s in range(half)]
        arrivals = [(0, (me % 2) ^ b, node ^ half ^ s, seconds[s]) for s in range(half)]
        early += arrivals if b == 0 else arrivals[:1]
        late = arrivals[1:]
    latents = finish(pieces, (1, 2), w3, g3, shape)
    latents = finish(early, (lines, 1), w3, g3, shape, latents)
    for piece in late:
        latents = finish([piece], (lines, 1), w3, g3, shape, latents)
    return latents.reshape(shares * nodes * CAP, latent, places // shares, c3)


def solution(mesh):
    return jax.shard_map(
        on_device,
        mesh=mesh,
        in_specs=(
            P(("clip", "patch"), None, None, None),
            P(("clip", "patch"), None),
            P(),
            P(),
            P(),
            P(),
            P(),
            P(),
        ),
        out_specs=P("clip", None, "patch", None),
        check_vma=False,
    )
```

```python
import functools

import jax
import jax.numpy as jnp
import ml_dtypes
import numpy as np
from jax import lax
from jax.experimental import pallas as pl
from jax.experimental.pallas import tpu as pltpu
from jax.sharding import PartitionSpec as P

GRID = 8
GROUPS = 32
CAP = 2
TILE = 16
PARTS = 3
BATCH = 4
NAMES = 2 * PARTS * GROUPS
F32, BF16 = jnp.float32, jnp.bfloat16


def spread_table(latent, chunk):
    table = np.zeros((3, chunk, latent, 2 * latent, chunk), np.float32)
    places = np.arange(chunk)
    for tap in range(3):
        for step in range(latent):
            if 2 * step - 1 + tap >= 0:
                table[tap, places, step, 2 * step - 1 + tap, places] = 1
    return table.reshape(3 * chunk * latent, 2 * latent * chunk)


def swap_table(latent, share):
    table = np.zeros((latent, share, share, latent), np.float32)
    for step in range(latent):
        table[step, np.arange(share), np.arange(share), step] = 1
    return table.reshape(latent * share, latent * share)


def fold_table(channels, lanes):
    width = channels // GROUPS
    group = np.arange(lanes) // width
    return (group[:, None] == group[None, :]).astype(np.float32) / width


def pick_table(channels):
    table = np.zeros((channels, 256), np.float32)
    lanes = np.arange(NAMES)
    table[lanes % GROUPS * (channels // GROUPS), lanes] = 1
    return table


def place_table(channels):
    table = np.zeros((256, 2, channels), np.float32)
    lanes = np.arange(NAMES)
    of_group = lanes[:, None] % GROUPS == np.arange(channels)[None, :] // (channels // GROUPS)
    for which in range(2):
        mine = lanes // (PARTS * GROUPS) == which
        table[:NAMES, which] = of_group & mine[:, None]
    return table.reshape(256, 2 * channels)


def stacked(tables):
    rows = [np.pad(t, ((0, 0), (0, 256 - t.shape[1]))) for t in tables]
    starts = np.cumsum([0] + [r.shape[0] for r in rows])
    return np.concatenate(rows).astype(ml_dtypes.bfloat16), [int(s) for s in starts]


def split(row):
    parts = []
    for _ in range(PARTS):
        head = row.astype(BF16)
        parts.append(head.astype(F32))
        row = row - head.astype(F32)
    return parts


def fold(rows, table):
    lanes = table.shape[0]
    halves = rows[0].shape[1] // lanes
    stack = []
    for row in rows:
        parts = split(row)
        stack += [part[:, h * lanes : (h + 1) * lanes] for h in range(halves) for part in parts]
    spare = -len(stack) % TILE
    if spare:
        stack.append(jnp.zeros((spare, lanes), F32))
    out = jnp.dot(jnp.concatenate(stack, axis=0).astype(BF16), table, preferred_element_type=F32)
    sums = []
    for k in range(0, len(rows) * halves, halves):
        at = [PARTS * (k + h) for h in range(halves)]
        sums.append(jnp.concatenate([jnp.sum(out[i : i + PARTS], axis=0, keepdims=True) for i in at], axis=1))
    return sums


def centre(values, table):
    share = 1.0 / values[0].shape[0]
    averages = fold([jnp.sum(v, axis=0, keepdims=True) * share for v in values], table)
    centred = [v - average for v, average in zip(values, averages)]
    powers = fold([jnp.sum(v * v, axis=0, keepdims=True) * share for v in centred], table)
    return averages, centred, [lax.rsqrt(power + 1e-05) for power in powers]


def silu(v):
    half = 0.5 * v
    return half + half * jnp.tanh(half)


def encode_kernel(named, x, *rest, starts, shares, owned):
    given, rest = rest[:6], rest[6:]
    sends, rest = rest[:shares], rest[shares:]
    (w1, g1, w2, g2, w3, tables), (tubes, wide, act, sems, tube_sems) = rest[:6], rest[6:]
    me = lax.axis_index("patch").astype(jnp.int32)
    copies = [pltpu.make_async_copy(a, b, sems.at[i]) for i, (a, b) in enumerate(zip(given, rest[:6]))]
    step = pl.program_id(0)

    def arrive(*which):
        @pl.when(step == 0)
        def _():
            for i in which:
                copies[i].wait()

    batch, frames, places, breadth = tubes.shape
    loads = [pltpu.make_async_copy(x.at[step * batch + b], tubes.at[b], tube_sems.at[b]) for b in range(batch)]
    latent = frames // 2
    c1, c2 = w1.shape[1], w2.shape[2]
    line = GRID * latent
    share = places * latent // shares
    chunk = 2 * GRID
    rows = places * latent

    @pl.when(step == 0)
    def _():
        copies[0].start()

    loads[0].start()

    @pl.when(step == 0)
    def _():
        copies[5].start()
        copies[1].start()

    for load in loads[1:]:
        load.start()

    @pl.when(step == 0)
    def _():
        for i in (2, 3, 4):
            copies[i].start()
        for b in range(batch):
            wide[b, 0:line, :] = jnp.zeros((line, wide.shape[2]), BF16)
            wide[b, (GRID + 1) * line :, :] = jnp.zeros((line, wide.shape[2]), BF16)

    arrive(0, 5, 1)
    spread = tables[starts[0] : starts[1]]
    swap = tables[starts[1] : starts[2], 0:share]
    fold1 = tables[starts[2] : starts[3], 0:c1]
    fold2 = tables[starts[3] : starts[4], 0:c2]
    fold3 = tables[starts[4] : starts[5]]
    pick = tables[starts[5] : starts[6]]
    first = []
    for b in range(batch):
        loads[b].wait()
        first.append(jnp.dot(tubes[b].reshape(frames * places, breadth), w1[...], preferred_element_type=F32))
    _, centred, scales = centre(first, fold1)
    for b in range(batch):
        act1 = silu(centred[b] * (scales[b] * g1[...])).astype(BF16).reshape(frames, places, c1)
        for q in range(places // chunk):
            block = act1[:, q * chunk : (q + 1) * chunk].reshape(frames * chunk, c1)
            taps = jnp.dot(spread, block, preferred_element_type=F32)
            taps = taps.reshape(3, chunk // GRID, GRID, latent, c1)
            edge = jnp.zeros((chunk // GRID, 1, latent, c1), F32)
            at = line + q * chunk * latent
            for a in range(3):
                for j in range(3):
                    tap = taps[a]
                    if j == 0:
                        tap = jnp.concatenate([edge, tap[:, : GRID - 1]], axis=1)
                    if j == 2:
                        tap = jnp.concatenate([tap[:, 1:], edge], axis=1)
                    tap = tap.reshape(chunk * latent, c1).astype(BF16)
                    wide[b, at : at + chunk * latent, (3 * j + a) * c1 : (3 * j + a + 1) * c1] = tap
    arrive(2, 3, 4)
    second = []
    for b in range(batch):
        total = jnp.dot(wide[b, 0:rows], w2[0], preferred_element_type=F32)
        for i in (1, 2):
            total += jnp.dot(wide[b, i * line : i * line + rows], w2[i], preferred_element_type=F32)
        second.append(total)
    _, centred, scales = centre(second, fold2)
    third = []
    for b in range(batch):
        act2 = silu(centred[b] * (scales[b] * g2[...])).astype(BF16)
        act[b] = act2
        third.append(jnp.dot(act2, w3[...], preferred_element_type=F32))
    averages, _, scales = centre(third, fold3)
    lane = lax.broadcasted_iota(jnp.int32, (1, 256), 1)
    row = lax.broadcasted_iota(jnp.int32, (TILE, 256), 0)
    parts = [part for b in range(batch) for part in split(averages[b]) + split(scales[b])]
    parts.append(jnp.zeros((-len(parts) % TILE, third[0].shape[1]), F32))
    picked = jnp.dot(jnp.concatenate(parts, axis=0).astype(BF16), pick, preferred_element_type=F32)
    names = jnp.zeros((1, 256), F32)
    for k in range(owned):
        names = jnp.where(lane == NAMES + k, named[k].astype(F32), names)
    notes = jnp.zeros((TILE, 256), F32)
    for b in range(batch):
        note = names
        for k in range(2 * PARTS):
            at = 2 * PARTS * b + k
            note = jnp.where(lane // GROUPS == k, picked[at : at + 1], note)
        notes = jnp.where(row == step * batch + b, note, notes)
    body = sends[0].shape[0] - TILE
    for j in range(shares):
        q = me ^ j
        for b in range(batch):
            part = act[b, pl.ds(pl.multiple_of(q * share, share), share), :]
            part = jnp.dot(swap, part, preferred_element_type=F32).astype(BF16)
            sends[j][pl.ds(pl.multiple_of((step * batch + b) * share, share), share), :] = part

        @pl.when(step == 0)
        def _():
            sends[j][body : body + TILE, :] = notes.astype(BF16)

        @pl.when(step > 0)
        def _():
            held = sends[j][body : body + TILE, :].astype(F32)
            sends[j][body : body + TILE, :] = (held + notes).astype(BF16)


def encode(named, pixels, weights, shares):
    w1, g1, w2, g2, w3 = weights
    owned, frames, places, breadth = pixels.shape
    latent = frames // 2
    c1, c2, c3 = w1.shape[1], w2.shape[2], w3.shape[1]
    share = latent * places // shares
    tables, starts = stacked([
        spread_table(latent, 2 * GRID),
        swap_table(latent, places // shares),
        fold_table(c1, c1),
        fold_table(c2, c2),
        fold_table(c3, 256),
        pick_table(c3),
    ])
    operands = [w1, g1.reshape(1, c1), w2.reshape(3, 3 * w2.shape[1], c2), g2.reshape(1, c2), w3]
    operands.append(jnp.asarray(tables))
    body = owned * share + TILE
    flops = 2 * frames * places * breadth * c1 + 2 * latent * places * (27 * c1 * c2 + c2 * c3)
    return pl.pallas_call(
        functools.partial(encode_kernel, starts=starts, shares=shares, owned=owned),
        grid_spec=pltpu.PrefetchScalarGridSpec(
            num_scalar_prefetch=1,
            grid=(owned // BATCH,),
            in_specs=[pl.BlockSpec(memory_space=pltpu.HBM)] * (1 + len(operands)),
            out_specs=[pl.BlockSpec((body, c2), lambda i, s: (0, 0))] * shares,
            scratch_shapes=[pltpu.VMEM(o.shape, o.dtype) for o in operands]
            + [
                pltpu.VMEM((BATCH, frames, places, breadth), BF16),
                pltpu.VMEM((BATCH, (GRID + 2) * GRID * latent, 9 * c1), BF16),
                pltpu.VMEM((BATCH, places * latent, c2), BF16),
                pltpu.SemaphoreType.DMA((len(operands),)),
                pltpu.SemaphoreType.DMA((BATCH,)),
            ],
        ),
        out_shape=[jax.ShapeDtypeStruct((body, c2), BF16)] * shares,
        compiler_params=pltpu.CompilerParams(vmem_limit_bytes=60 * 1024 * 1024),
        cost_estimate=pl.CostEstimate(
            flops=owned * flops, bytes_accessed=owned * frames * places * breadth * 2, transcendentals=0
        ),
        name="encode",
    )(named, pixels, *operands)


def pack_kernel(ints, *rest, half, jobs, pick, owned, share):
    arrays = sum(len(job) for job in jobs)
    held, outs = rest[:arrays], rest[arrays:]
    me = lax.axis_index("patch").astype(jnp.int32)
    node = lax.axis_index("clip").astype(jnp.int32)
    owners = len(jobs[0])
    body = owned * share
    notes = jnp.concatenate([held[k][body : body + TILE, :] for k in range(owners)], axis=0)
    width = owners * TILE
    rows = lax.broadcasted_iota(jnp.int32, (TILE, width), 0)
    columns = lax.broadcasted_iota(jnp.int32, (TILE, width), 1)
    for s in range(half):
        sel = jnp.zeros((TILE, width), jnp.bool_)
        for j in range(owners):
            seen = jnp.int32(0)
            found = [jnp.int32(0)] * CAP
            for i in range(owned):
                mine = ints[j * owned + i] == (node ^ s)
                for r in range(CAP):
                    found[r] = jnp.where(mine & (seen == r), i, found[r])
                seen = seen + mine.astype(jnp.int32)
            for r in range(CAP):
                row = pick(me ^ jobs[0][j]) * CAP + r
                to = pl.ds(pl.multiple_of(row * share, share), share)
                at = pl.ds(pl.multiple_of(found[r] * share, share), share)
                sel = sel | ((rows == jnp.where(seen > r, row, -1)) & (columns == j * TILE + found[r]))
                for g in range(len(jobs)):
                    outs[g * half + s][to, :] = held[g * owners + j][at, :]
        sel = jnp.where(sel, 1.0, 0.0).astype(BF16)
        ready = jnp.dot(sel, notes, preferred_element_type=F32).astype(BF16)
        for g in range(len(jobs)):
            outs[g * half + s][owners * CAP * share :, :] = ready


def pack(half, held, jobs, pick, owned, share):
    owners, channels = len(jobs[0]), held[0].shape[1]
    names = [h[owned * share, NAMES : NAMES + owned] for h in held[:owners]]
    ints = jnp.concatenate(names).astype(jnp.int32)
    out_rows = owners * CAP * share + TILE
    count = len(jobs) * half
    outs = pl.pallas_call(
        functools.partial(pack_kernel, half=half, jobs=jobs, pick=pick, owned=owned, share=share),
        grid_spec=pltpu.PrefetchScalarGridSpec(
            num_scalar_prefetch=1,
            grid=(1,),
            in_specs=[pl.BlockSpec(h.shape, lambda i, s: (0, 0)) for h in held],
            out_specs=[pl.BlockSpec((out_rows, channels), lambda i, s: (0, 0))] * count,
        ),
        out_shape=[jax.ShapeDtypeStruct((out_rows, channels), BF16)] * count,
        compiler_params=pltpu.CompilerParams(vmem_limit_bytes=16 * 1024 * 1024),
        cost_estimate=pl.CostEstimate(flops=0, bytes_accessed=2 * count * out_rows * channels, transcendentals=0),
        name="pack",
    )(ints, *held)
    return [outs[g * half : (g + 1) * half] for g in range(len(jobs))]


def finish_kernel(places, w3, g3, place, *rest, count):
    taken, out = rest[:count], rest[-1]
    c3 = w3.shape[1]
    lines, cores, _, cap, latent, share, _ = out.shape
    rows = latent * share
    owners = [(y, core) for y in range(lines) for core in range(cores)]
    for i in range(count):

        @pl.when(pl.program_id(0) == i)
        def _():
            wide = jnp.dot(taken[i][len(owners) * cap * rows :, :], place[...], preferred_element_type=F32)
            mean, gain = wide[:, :c3], wide[:, c3:] * g3[...]
            for p, (y, core) in enumerate(owners):
                block = taken[i][p * cap * rows : (p + 1) * cap * rows, :]
                third = jnp.dot(block, w3[...], preferred_element_type=F32)
                for r in range(cap):
                    at = p * cap + r
                    token = (third[r * rows : (r + 1) * rows] - mean[at : at + 1]) * gain[at : at + 1]
                    out[y, core, 0, r] = token.reshape(latent, share, c3).astype(BF16)


def finish(pieces, block, w3, g3, shape, before=None):
    count = len(pieces)
    cap, latent, share, c3 = shape[3:]
    rows = latent * share
    c2 = w3.shape[0]
    arrays = [piece[3] for piece in pieces]
    places = jnp.stack([jnp.asarray(piece[k], jnp.int32) for piece in pieces for k in range(3)])
    place = jnp.asarray(place_table(c3).astype(ml_dtypes.bfloat16))
    operands = [w3, g3, place, *arrays]
    specs = [pl.BlockSpec(o.shape, lambda k, s: (0, 0)) for o in operands]
    aliases = {}
    if before is not None:
        specs.append(pl.BlockSpec(memory_space=pl.ANY))
        aliases = {1 + len(operands): 0}
        operands.append(before)
    blocks = count * block[0] * block[1] * cap
    return pl.pallas_call(
        functools.partial(finish_kernel, count=count),
        grid_spec=pltpu.PrefetchScalarGridSpec(
            num_scalar_prefetch=1,
            grid=(count,),
            in_specs=specs,
            out_specs=pl.BlockSpec(
                (*block, 1, cap, latent, share, c3),
                lambda k, s: (s[3 * k], s[3 * k + 1], s[3 * k + 2], 0, 0, 0, 0),
            ),
        ),
        out_shape=jax.ShapeDtypeStruct(shape, BF16),
        input_output_aliases=aliases,
        compiler_params=pltpu.CompilerParams(vmem_limit_bytes=24 * 1024 * 1024),
        cost_estimate=pl.CostEstimate(
            flops=2 * blocks * rows * c2 * c3, bytes_accessed=blocks * rows * (c2 + c3) * 2, transcendentals=0
        ),
        name="finish",
    )(places, *operands)


def on_device(pixels, destination, embed_weight, embed_gain, mixing_weight, mixing_gain, project_weight, project_gain):
    nodes, shares = lax.axis_size("clip"), lax.axis_size("patch")
    node = lax.axis_index("clip").astype(jnp.int32)
    half = nodes // 2
    owned, frames, places, _ = pixels.shape
    latent, c3 = frames // 2, project_weight.shape[1]
    share = latent * places // shares
    weights = (embed_weight, embed_gain, mixing_weight, mixing_gain, project_weight)
    named = destination.reshape(owned)

    me = lax.axis_index("patch").astype(jnp.int32)
    lines = shares // 2
    w3, g3 = project_weight, project_gain.reshape(1, c3)
    shape = (lines, 2, nodes, CAP, latent, places // shares, c3)

    def send(array, s, j):
        if s == 0 and j == 0:
            return array
        pairs = [(c * shares + p, (c ^ s) * shares + (p ^ j)) for c in range(nodes) for p in range(shares)]
        return lax.ppermute(array, ("clip", "patch"), pairs)

    sends = encode(named, pixels, weights, shares)
    held = [sends[0::2], [send(array, 0, 1) for array in sends[1::2]]]
    pairs = [[held[0][k], held[1][k]] for k in range(lines)]
    own = pack(half, [a for pair in pairs for a in pair], [[0, 1]] * lines, lambda p: p % 2, owned, share)
    def after(arrays, *earlier):
        return list(lax.optimization_barrier((*arrays, *earlier))[: len(arrays)])

    crossed = [send(held[0][k], half, 2 * k) for k in range(lines)]
    arrived = [[send(own[k][s], s, 2 * k) for s in range(half)] for k in range(lines)]
    pieces = [((me // 2) ^ k, 0, node ^ s, arrived[k][s]) for k in range(lines) for s in range(half)]
    beyond = after(held[1], *crossed, *[a for line in own for a in line], arrived[0][1])
    beyond = [send(beyond[k], half, 2 * k) for k in range(lines)]
    early, late = [], []
    for b, far in enumerate((crossed, beyond)):
        if b:
            far = after(far, *[a for line in arrived[1:] for a in line], *arrived[0])
        (other,) = pack(half, far, [[2 * k + b for k in range(lines)]], lambda p: p // 2, owned, share)
        arrivals = [(0, (me % 2) ^ b, node ^ half ^ s, send(other[s], s, 0)) for s in range(half)]
        early += arrivals if b == 0 else arrivals[:1]
        late = arrivals[1:]
    latents = finish(pieces, (1, 2), w3, g3, shape)
    latents = finish(early, (lines, 1), w3, g3, shape, latents)
    latents = finish(late, (lines, 1), w3, g3, shape, latents)
    return latents.reshape(shares * nodes * CAP, latent, places // shares, c3)


def solution(mesh):
    return jax.shard_map(
        on_device,
        mesh=mesh,
        in_specs=(
            P(("clip", "patch"), None, None, None),
            P(("clip", "patch"), None),
            P(),
            P(),
            P(),
            P(),
            P(),
            P(),
        ),
        out_specs=P("clip", None, "patch", None),
        check_vma=False,
    )
```

```python
import functools

import jax
import jax.numpy as jnp
import ml_dtypes
import numpy as np
from jax import lax
from jax.experimental import pallas as pl
from jax.experimental.pallas import tpu as pltpu
from jax.sharding import PartitionSpec as P

GRID = 8
GROUPS = 32
CAP = 2
TILE = 16
PARTS = 3
BATCH = 4
NAMES = 2 * PARTS * GROUPS
F32, BF16 = jnp.float32, jnp.bfloat16


def spread_table(latent, chunk):
    table = np.zeros((3, chunk, latent, 2 * latent, chunk), np.float32)
    places = np.arange(chunk)
    for tap in range(3):
        for step in range(latent):
            if 2 * step - 1 + tap >= 0:
                table[tap, places, step, 2 * step - 1 + tap, places] = 1
    return table.reshape(3 * chunk * latent, 2 * latent * chunk)


def swap_table(latent, share):
    table = np.zeros((latent, share, share, latent), np.float32)
    for step in range(latent):
        table[step, np.arange(share), np.arange(share), step] = 1
    return table.reshape(latent * share, latent * share)


def fold_table(channels, lanes):
    width = channels // GROUPS
    group = np.arange(lanes) // width
    return (group[:, None] == group[None, :]).astype(np.float32) / width


def pick_table(channels):
    table = np.zeros((channels, 256), np.float32)
    lanes = np.arange(NAMES)
    table[lanes % GROUPS * (channels // GROUPS), lanes] = 1
    return table


def place_table(channels):
    table = np.zeros((256, 2, channels), np.float32)
    lanes = np.arange(NAMES)
    of_group = lanes[:, None] % GROUPS == np.arange(channels)[None, :] // (channels // GROUPS)
    for which in range(2):
        mine = lanes // (PARTS * GROUPS) == which
        table[:NAMES, which] = of_group & mine[:, None]
    return table.reshape(256, 2 * channels)


def stacked(tables):
    rows = [np.pad(t, ((0, 0), (0, 256 - t.shape[1]))) for t in tables]
    starts = np.cumsum([0] + [r.shape[0] for r in rows])
    return np.concatenate(rows).astype(ml_dtypes.bfloat16), [int(s) for s in starts]


def split(row):
    parts = []
    for _ in range(PARTS):
        head = row.astype(BF16)
        parts.append(head.astype(F32))
        row = row - head.astype(F32)
    return parts


def fold(rows, table):
    lanes = table.shape[0]
    halves = rows[0].shape[1] // lanes
    stack = []
    for row in rows:
        parts = split(row)
        stack += [part[:, h * lanes : (h + 1) * lanes] for h in range(halves) for part in parts]
    spare = -len(stack) % TILE
    if spare:
        stack.append(jnp.zeros((spare, lanes), F32))
    out = jnp.dot(jnp.concatenate(stack, axis=0).astype(BF16), table, preferred_element_type=F32)
    sums = []
    for k in range(0, len(rows) * halves, halves):
        at = [PARTS * (k + h) for h in range(halves)]
        sums.append(jnp.concatenate([jnp.sum(out[i : i + PARTS], axis=0, keepdims=True) for i in at], axis=1))
    return sums


def centre(values, table):
    share = 1.0 / values[0].shape[0]
    averages = fold([jnp.sum(v, axis=0, keepdims=True) * share for v in values], table)
    centred = [v - average for v, average in zip(values, averages)]
    powers = fold([jnp.sum(v * v, axis=0, keepdims=True) * share for v in centred], table)
    return averages, centred, [lax.rsqrt(power + 1e-05) for power in powers]


def silu(v):
    half = 0.5 * v
    return half + half * jnp.tanh(half)


def encode_kernel(named, x, *rest, starts, shares, owned):
    given, rest = rest[:6], rest[6:]
    sends, rest = rest[:shares], rest[shares:]
    (w1, g1, w2, g2, w3, tables), (tubes, wide, act, sems, tube_sems) = rest[:6], rest[6:]
    me = lax.axis_index("patch").astype(jnp.int32)
    copies = [pltpu.make_async_copy(a, b, sems.at[i]) for i, (a, b) in enumerate(zip(given, rest[:6]))]
    step = pl.program_id(0)

    def arrive(*which):
        @pl.when(step == 0)
        def _():
            for i in which:
                copies[i].wait()

    batch, frames, places, breadth = tubes.shape
    loads = [pltpu.make_async_copy(x.at[step * batch + b], tubes.at[b], tube_sems.at[b]) for b in range(batch)]
    latent = frames // 2
    c1, c2 = w1.shape[1], w2.shape[2]
    line = GRID * latent
    share = places * latent // shares
    chunk = 2 * GRID
    rows = places * latent

    @pl.when(step == 0)
    def _():
        copies[0].start()

    loads[0].start()

    @pl.when(step == 0)
    def _():
        copies[5].start()
        copies[1].start()

    for load in loads[1:]:
        load.start()

    @pl.when(step == 0)
    def _():
        for i in (2, 3, 4):
            copies[i].start()
        for b in range(batch):
            wide[b, 0:line, :] = jnp.zeros((line, wide.shape[2]), BF16)
            wide[b, (GRID + 1) * line :, :] = jnp.zeros((line, wide.shape[2]), BF16)

    arrive(0, 5, 1)
    spread = tables[starts[0] : starts[1]]
    swap = tables[starts[1] : starts[2], 0:share]
    fold1 = tables[starts[2] : starts[3], 0:c1]
    fold2 = tables[starts[3] : starts[4], 0:c2]
    fold3 = tables[starts[4] : starts[5]]
    pick = tables[starts[5] : starts[6]]
    first = []
    for b in range(batch):
        loads[b].wait()
        first.append(jnp.dot(tubes[b].reshape(frames * places, breadth), w1[...], preferred_element_type=F32))
    _, centred, scales = centre(first, fold1)
    for b in range(batch):
        act1 = silu(centred[b] * (scales[b] * g1[...])).astype(BF16).reshape(frames, places, c1)
        for q in range(places // chunk):
            block = act1[:, q * chunk : (q + 1) * chunk].reshape(frames * chunk, c1)
            taps = jnp.dot(spread, block, preferred_element_type=F32)
            taps = taps.reshape(3, chunk // GRID, GRID, latent, c1)
            edge = jnp.zeros((chunk // GRID, 1, latent, c1), F32)
            at = line + q * chunk * latent
            for a in range(3):
                for j in range(3):
                    tap = taps[a]
                    if j == 0:
                        tap = jnp.concatenate([edge, tap[:, : GRID - 1]], axis=1)
                    if j == 2:
                        tap = jnp.concatenate([tap[:, 1:], edge], axis=1)
                    tap = tap.reshape(chunk * latent, c1).astype(BF16)
                    wide[b, at : at + chunk * latent, (3 * j + a) * c1 : (3 * j + a + 1) * c1] = tap
    arrive(2, 3, 4)
    second = []
    for b in range(batch):
        total = jnp.dot(wide[b, 0:rows], w2[0], preferred_element_type=F32)
        for i in (1, 2):
            total += jnp.dot(wide[b, i * line : i * line + rows], w2[i], preferred_element_type=F32)
        second.append(total)
    _, centred, scales = centre(second, fold2)
    third = []
    for b in range(batch):
        act2 = silu(centred[b] * (scales[b] * g2[...])).astype(BF16)
        act[b] = act2
        third.append(jnp.dot(act2, w3[...], preferred_element_type=F32))
    averages, _, scales = centre(third, fold3)
    lane = lax.broadcasted_iota(jnp.int32, (1, 256), 1)
    row = lax.broadcasted_iota(jnp.int32, (TILE, 256), 0)
    parts = [part for b in range(batch) for part in split(averages[b]) + split(scales[b])]
    parts.append(jnp.zeros((-len(parts) % TILE, third[0].shape[1]), F32))
    picked = jnp.dot(jnp.concatenate(parts, axis=0).astype(BF16), pick, preferred_element_type=F32)
    names = jnp.zeros((1, 256), F32)
    for k in range(owned):
        names = jnp.where(lane == NAMES + k, named[k].astype(F32), names)
    notes = jnp.zeros((TILE, 256), F32)
    for b in range(batch):
        note = names
        for k in range(2 * PARTS):
            at = 2 * PARTS * b + k
            note = jnp.where(lane // GROUPS == k, picked[at : at + 1], note)
        notes = jnp.where(row == step * batch + b, note, notes)
    body = sends[0].shape[0] - TILE
    for j in range(shares):
        q = me ^ j
        for b in range(batch):
            part = act[b, pl.ds(pl.multiple_of(q * share, share), share), :]
            part = jnp.dot(swap, part, preferred_element_type=F32).astype(BF16)
            sends[j][pl.ds(pl.multiple_of((step * batch + b) * share, share), share), :] = part

        @pl.when(step == 0)
        def _():
            sends[j][body : body + TILE, :] = notes.astype(BF16)

        @pl.when(step > 0)
        def _():
            held = sends[j][body : body + TILE, :].astype(F32)
            sends[j][body : body + TILE, :] = (held + notes).astype(BF16)


def encode(named, pixels, weights, shares):
    w1, g1, w2, g2, w3 = weights
    owned, frames, places, breadth = pixels.shape
    latent = frames // 2
    c1, c2, c3 = w1.shape[1], w2.shape[2], w3.shape[1]
    share = latent * places // shares
    tables, starts = stacked([
        spread_table(latent, 2 * GRID),
        swap_table(latent, places // shares),
        fold_table(c1, c1),
        fold_table(c2, c2),
        fold_table(c3, 256),
        pick_table(c3),
    ])
    operands = [w1, g1.reshape(1, c1), w2.reshape(3, 3 * w2.shape[1], c2), g2.reshape(1, c2), w3]
    operands.append(jnp.asarray(tables))
    body = owned * share + TILE
    flops = 2 * frames * places * breadth * c1 + 2 * latent * places * (27 * c1 * c2 + c2 * c3)
    return pl.pallas_call(
        functools.partial(encode_kernel, starts=starts, shares=shares, owned=owned),
        grid_spec=pltpu.PrefetchScalarGridSpec(
            num_scalar_prefetch=1,
            grid=(owned // BATCH,),
            in_specs=[pl.BlockSpec(memory_space=pltpu.HBM)] * (1 + len(operands)),
            out_specs=[pl.BlockSpec((body, c2), lambda i, s: (0, 0))] * shares,
            scratch_shapes=[pltpu.VMEM(o.shape, o.dtype) for o in operands]
            + [
                pltpu.VMEM((BATCH, frames, places, breadth), BF16),
                pltpu.VMEM((BATCH, (GRID + 2) * GRID * latent, 9 * c1), BF16),
                pltpu.VMEM((BATCH, places * latent, c2), BF16),
                pltpu.SemaphoreType.DMA((len(operands),)),
                pltpu.SemaphoreType.DMA((BATCH,)),
            ],
        ),
        out_shape=[jax.ShapeDtypeStruct((body, c2), BF16)] * shares,
        compiler_params=pltpu.CompilerParams(vmem_limit_bytes=44 * 1024 * 1024),
        cost_estimate=pl.CostEstimate(
            flops=owned * flops, bytes_accessed=owned * frames * places * breadth * 2, transcendentals=0
        ),
        name="encode",
    )(named, *[pltpu.with_memory_space_constraint(o, pltpu.HBM) for o in (pixels, *operands)])


def pack_kernel(ints, *rest, half, jobs, pick, owned, share):
    arrays = sum(len(job) for job in jobs)
    held, outs = rest[:arrays], rest[arrays:]
    me = lax.axis_index("patch").astype(jnp.int32)
    node = lax.axis_index("clip").astype(jnp.int32)
    owners = len(jobs[0])
    body = owned * share
    notes = jnp.concatenate([held[k][body : body + TILE, :] for k in range(owners)], axis=0)
    width = owners * TILE
    rows = lax.broadcasted_iota(jnp.int32, (TILE, width), 0)
    columns = lax.broadcasted_iota(jnp.int32, (TILE, width), 1)
    for s in range(half):
        sel = jnp.zeros((TILE, width), jnp.bool_)
        for j in range(owners):
            seen = jnp.int32(0)
            found = [jnp.int32(0)] * CAP
            for i in range(owned):
                mine = ints[j * owned + i] == (node ^ s)
                for r in range(CAP):
                    found[r] = jnp.where(mine & (seen == r), i, found[r])
                seen = seen + mine.astype(jnp.int32)
            for r in range(CAP):
                row = pick(me ^ jobs[0][j]) * CAP + r
                to = pl.ds(pl.multiple_of(row * share, share), share)
                at = pl.ds(pl.multiple_of(found[r] * share, share), share)
                sel = sel | ((rows == jnp.where(seen > r, row, -1)) & (columns == j * TILE + found[r]))
                for g in range(len(jobs)):
                    outs[g * half + s][to, :] = held[g * owners + j][at, :]
        sel = jnp.where(sel, 1.0, 0.0).astype(BF16)
        ready = jnp.dot(sel, notes, preferred_element_type=F32).astype(BF16)
        for g in range(len(jobs)):
            outs[g * half + s][owners * CAP * share :, :] = ready


def pack(half, held, jobs, pick, owned, share):
    owners, channels = len(jobs[0]), held[0].shape[1]
    names = [h[owned * share, NAMES : NAMES + owned] for h in held[:owners]]
    ints = jnp.concatenate(names).astype(jnp.int32)
    out_rows = owners * CAP * share + TILE
    count = len(jobs) * half
    outs = pl.pallas_call(
        functools.partial(pack_kernel, half=half, jobs=jobs, pick=pick, owned=owned, share=share),
        grid_spec=pltpu.PrefetchScalarGridSpec(
            num_scalar_prefetch=1,
            grid=(1,),
            in_specs=[pl.BlockSpec(h.shape, lambda i, s: (0, 0)) for h in held],
            out_specs=[pl.BlockSpec((out_rows, channels), lambda i, s: (0, 0))] * count,
        ),
        out_shape=[jax.ShapeDtypeStruct((out_rows, channels), BF16)] * count,
        compiler_params=pltpu.CompilerParams(vmem_limit_bytes=16 * 1024 * 1024),
        cost_estimate=pl.CostEstimate(flops=0, bytes_accessed=2 * count * out_rows * channels, transcendentals=0),
        name="pack",
    )(ints, *held)
    return [outs[g * half : (g + 1) * half] for g in range(len(jobs))]


def finish_kernel(places, w3, g3, place, *rest, count):
    taken, (out, ready, sems) = rest[:count], rest[-3:]
    c3 = w3.shape[1]
    _, lines, cores, _, cap, latent, share, _ = ready.shape
    rows = latent * share
    owners = [(line, core) for line in range(lines) for core in range(cores)]
    tail = len(owners) * cap * rows
    notes = jnp.concatenate([taken[i][tail : tail + TILE, :] for i in range(count)], axis=0)
    wide = jnp.dot(notes, place[...], preferred_element_type=F32)
    mean, gain = wide[:, :c3], wide[:, c3:] * g3[...]
    copies = []
    for i in range(count):
        for p, (line, core) in enumerate(owners):
            block = taken[i][p * cap * rows : (p + 1) * cap * rows, :]
            third = jnp.dot(block, w3[...], preferred_element_type=F32)
            for r in range(cap):
                at = i * TILE + p * cap + r
                token = (third[r * rows : (r + 1) * rows] - mean[at : at + 1]) * gain[at : at + 1]
                ready[i, line, core, 0, r] = token.reshape(latent, share, c3).astype(BF16)
        spot = out.at[
            pl.ds(places[3 * i] * lines, lines), pl.ds(places[3 * i + 1] * cores, cores), pl.ds(places[3 * i + 2], 1)
        ]
        copies.append(pltpu.make_async_copy(ready.at[i], spot, sems.at[i]))
        copies[i].start()
    for copy in copies:
        copy.wait()


def finish(pieces, block, w3, g3, shape, before=None):
    count = len(pieces)
    cap, latent, share, c3 = shape[3:]
    rows = latent * share
    c2 = w3.shape[0]
    arrays = [piece[3] for piece in pieces]
    places = jnp.stack([jnp.asarray(piece[k], jnp.int32) for piece in pieces for k in range(3)])
    place = jnp.asarray(place_table(c3).astype(ml_dtypes.bfloat16))
    operands = [w3, g3, place, *arrays]
    specs = [pl.BlockSpec(o.shape, lambda k, s: (0, 0)) for o in operands]
    aliases = {}
    if before is not None:
        specs.append(pl.BlockSpec(memory_space=pl.ANY))
        aliases = {1 + len(operands): 0}
        operands.append(before)
    blocks = count * block[0] * block[1] * cap
    return pl.pallas_call(
        functools.partial(finish_kernel, count=count),
        grid_spec=pltpu.PrefetchScalarGridSpec(
            num_scalar_prefetch=1,
            grid=(1,),
            in_specs=specs,
            out_specs=pl.BlockSpec(memory_space=pl.ANY),
            scratch_shapes=[
                pltpu.VMEM((count, *block, 1, cap, latent, share, c3), BF16),
                pltpu.SemaphoreType.DMA((count,)),
            ],
        ),
        out_shape=jax.ShapeDtypeStruct(shape, BF16),
        input_output_aliases=aliases,
        compiler_params=pltpu.CompilerParams(vmem_limit_bytes=24 * 1024 * 1024),
        cost_estimate=pl.CostEstimate(
            flops=2 * blocks * rows * c2 * c3, bytes_accessed=blocks * rows * (c2 + c3) * 2, transcendentals=0
        ),
        name="finish",
    )(places, *operands)


def on_device(pixels, destination, embed_weight, embed_gain, mixing_weight, mixing_gain, project_weight, project_gain):
    nodes, shares = lax.axis_size("clip"), lax.axis_size("patch")
    node = lax.axis_index("clip").astype(jnp.int32)
    half = nodes // 2
    owned, frames, places, _ = pixels.shape
    latent, c3 = frames // 2, project_weight.shape[1]
    share = latent * places // shares
    weights = (embed_weight, embed_gain, mixing_weight, mixing_gain, project_weight)
    named = destination.reshape(owned)

    me = lax.axis_index("patch").astype(jnp.int32)
    lines = shares // 2
    w3, g3 = project_weight, project_gain.reshape(1, c3)
    shape = (lines, 2, nodes, CAP, latent, places // shares, c3)

    def send(array, s, j):
        if s == 0 and j == 0:
            return array
        pairs = [(c * shares + p, (c ^ s) * shares + (p ^ j)) for c in range(nodes) for p in range(shares)]
        return lax.ppermute(array, ("clip", "patch"), pairs)

    sends = encode(named, pixels, weights, shares)
    held = [sends[0::2], [send(array, 0, 1) for array in sends[1::2]]]
    pairs = [[held[0][k], held[1][k]] for k in range(lines)]
    own = pack(half, [a for pair in pairs for a in pair], [[0, 1]] * lines, lambda p: p % 2, owned, share)
    def after(arrays, *earlier):
        return list(lax.optimization_barrier((*arrays, *earlier))[: len(arrays)])

    crossed = [send(held[0][k], half, 2 * k) for k in range(lines)]
    arrived = [[send(own[k][s], s, 2 * k) for s in range(half)] for k in range(lines)]
    pieces = [((me // 2) ^ k, 0, node ^ s, arrived[k][s]) for k in range(lines) for s in range(half)]
    beyond = after(held[1], *crossed, *[a for line in own for a in line], arrived[1][half - 1])
    beyond = [send(beyond[k], half, 2 * k) for k in range(lines)]
    early, late = [], []
    for b, far in enumerate((crossed, beyond)):
        if b:
            far = after(far, *[a for line in arrived[1:] for a in line], *arrived[0])
        (other,) = pack(half, far, [[2 * k + b for k in range(lines)]], lambda p: p // 2, owned, share)
        arrivals = [(0, (me % 2) ^ b, node ^ half ^ s, send(other[s], s, 0)) for s in range(half)]
        early += arrivals if b == 0 else arrivals[:1]
        late = arrivals[1:]
    latents = finish(pieces, (1, 2), w3, g3, shape)
    latents = finish(early, (lines, 1), w3, g3, shape, latents)
    latents = finish(late, (lines, 1), w3, g3, shape, latents)
    return latents.reshape(shares * nodes * CAP, latent, places // shares, c3)


def solution(mesh):
    return jax.shard_map(
        on_device,
        mesh=mesh,
        in_specs=(
            P(("clip", "patch"), None, None, None),
            P(("clip", "patch"), None),
            P(),
            P(),
            P(),
            P(),
            P(),
            P(),
        ),
        out_specs=P("clip", None, "patch", None),
        check_vma=False,
    )
```

```python
import functools

import jax
import jax.numpy as jnp
import ml_dtypes
import numpy as np
from jax import lax
from jax.experimental import pallas as pl
from jax.experimental.pallas import tpu as pltpu
from jax.sharding import PartitionSpec as P

GRID = 8
GROUPS = 32
CAP = 2
TILE = 16
PARTS = 3
BATCH = 4
NAMES = 2 * PARTS * GROUPS
F32, BF16 = jnp.float32, jnp.bfloat16


def spread_table(latent, chunk):
    table = np.zeros((3, chunk, latent, 2 * latent, chunk), np.float32)
    places = np.arange(chunk)
    for tap in range(3):
        for step in range(latent):
            if 2 * step - 1 + tap >= 0:
                table[tap, places, step, 2 * step - 1 + tap, places] = 1
    return table.reshape(3 * chunk * latent, 2 * latent * chunk)


def swap_table(latent, share):
    table = np.zeros((latent, share, share, latent), np.float32)
    for step in range(latent):
        table[step, np.arange(share), np.arange(share), step] = 1
    return table.reshape(latent * share, latent * share)


def fold_table(channels, lanes):
    width = channels // GROUPS
    group = np.arange(lanes) // width
    return (group[:, None] == group[None, :]).astype(np.float32) / width


def pick_table(channels):
    table = np.zeros((channels, 256), np.float32)
    lanes = np.arange(NAMES)
    table[lanes % GROUPS * (channels // GROUPS), lanes] = 1
    return table


def place_table(channels):
    table = np.zeros((256, 2, channels), np.float32)
    lanes = np.arange(NAMES)
    of_group = lanes[:, None] % GROUPS == np.arange(channels)[None, :] // (channels // GROUPS)
    for which in range(2):
        mine = lanes // (PARTS * GROUPS) == which
        table[:NAMES, which] = of_group & mine[:, None]
    return table.reshape(256, 2 * channels)


def stacked(tables):
    rows = [np.pad(t, ((0, 0), (0, 256 - t.shape[1]))) for t in tables]
    starts = np.cumsum([0] + [r.shape[0] for r in rows])
    return np.concatenate(rows).astype(ml_dtypes.bfloat16), [int(s) for s in starts]


def split(row):
    parts = []
    for _ in range(PARTS):
        head = row.astype(BF16)
        parts.append(head.astype(F32))
        row = row - head.astype(F32)
    return parts


def fold(rows, table):
    lanes = table.shape[0]
    halves = rows[0].shape[1] // lanes
    stack = []
    for row in rows:
        parts = split(row)
        stack += [part[:, h * lanes : (h + 1) * lanes] for h in range(halves) for part in parts]
    spare = -len(stack) % TILE
    if spare:
        stack.append(jnp.zeros((spare, lanes), F32))
    out = jnp.dot(jnp.concatenate(stack, axis=0).astype(BF16), table, preferred_element_type=F32)
    sums = []
    for k in range(0, len(rows) * halves, halves):
        at = [PARTS * (k + h) for h in range(halves)]
        sums.append(jnp.concatenate([jnp.sum(out[i : i + PARTS], axis=0, keepdims=True) for i in at], axis=1))
    return sums


def centre(values, table):
    share = 1.0 / values[0].shape[0]
    averages = fold([jnp.sum(v, axis=0, keepdims=True) * share for v in values], table)
    centred = [v - average for v, average in zip(values, averages)]
    powers = fold([jnp.sum(v * v, axis=0, keepdims=True) * share for v in centred], table)
    return averages, centred, [lax.rsqrt(power + 1e-05) for power in powers]


def silu(v):
    half = 0.5 * v
    return half + half * jnp.tanh(half)


def encode_kernel(named, x, *rest, starts, shares, owned):
    given, rest = rest[:6], rest[6:]
    sends, rest = rest[:shares], rest[shares:]
    (w1, g1, w2, g2, w3, tables), (tubes, wide, act, sems, tube_sems) = rest[:6], rest[6:]
    me = lax.axis_index("patch").astype(jnp.int32)
    copies = [pltpu.make_async_copy(a, b, sems.at[i]) for i, (a, b) in enumerate(zip(given, rest[:6]))]
    step = pl.program_id(0)

    def arrive(*which):
        @pl.when(step == 0)
        def _():
            for i in which:
                copies[i].wait()

    batch, frames, places, breadth = tubes.shape
    loads = [pltpu.make_async_copy(x.at[step * batch + b], tubes.at[b], tube_sems.at[b]) for b in range(batch)]
    latent = frames // 2
    c1, c2 = w1.shape[1], w2.shape[2]
    line = GRID * latent
    share = places * latent // shares
    chunk = 2 * GRID
    rows = places * latent

    @pl.when(step == 0)
    def _():
        copies[0].start()

    loads[0].start()

    @pl.when(step == 0)
    def _():
        copies[5].start()
        copies[1].start()

    for load in loads[1:]:
        load.start()

    @pl.when(step == 0)
    def _():
        for i in (2, 3, 4):
            copies[i].start()
        for b in range(batch):
            wide[b, 0:line, :] = jnp.zeros((line, wide.shape[2]), BF16)
            wide[b, (GRID + 1) * line :, :] = jnp.zeros((line, wide.shape[2]), BF16)

    arrive(0, 5, 1)
    spread = tables[starts[0] : starts[1]]
    swap = tables[starts[1] : starts[2], 0:share]
    fold1 = tables[starts[2] : starts[3], 0:c1]
    fold2 = tables[starts[3] : starts[4], 0:c2]
    fold3 = tables[starts[4] : starts[5]]
    pick = tables[starts[5] : starts[6]]
    first = []
    for b in range(batch):
        loads[b].wait()
        first.append(jnp.dot(tubes[b].reshape(frames * places, breadth), w1[...], preferred_element_type=F32))
    _, centred, scales = centre(first, fold1)
    for b in range(batch):
        act1 = silu(centred[b] * (scales[b] * g1[...])).astype(BF16).reshape(frames, places, c1)
        for q in range(places // chunk):
            block = act1[:, q * chunk : (q + 1) * chunk].reshape(frames * chunk, c1)
            taps = jnp.dot(spread, block, preferred_element_type=F32)
            taps = taps.reshape(3, chunk // GRID, GRID, latent, c1)
            edge = jnp.zeros((chunk // GRID, 1, latent, c1), F32)
            at = line + q * chunk * latent
            for a in range(3):
                for j in range(3):
                    tap = taps[a]
                    if j == 0:
                        tap = jnp.concatenate([edge, tap[:, : GRID - 1]], axis=1)
                    if j == 2:
                        tap = jnp.concatenate([tap[:, 1:], edge], axis=1)
                    tap = tap.reshape(chunk * latent, c1).astype(BF16)
                    wide[b, at : at + chunk * latent, (3 * j + a) * c1 : (3 * j + a + 1) * c1] = tap
    arrive(2, 3, 4)
    second = []
    for b in range(batch):
        total = jnp.dot(wide[b, 0:rows], w2[0], preferred_element_type=F32)
        for i in (1, 2):
            total += jnp.dot(wide[b, i * line : i * line + rows], w2[i], preferred_element_type=F32)
        second.append(total)
    _, centred, scales = centre(second, fold2)
    third = []
    for b in range(batch):
        act2 = silu(centred[b] * (scales[b] * g2[...])).astype(BF16)
        act[b] = act2
        third.append(jnp.dot(act2, w3[...], preferred_element_type=F32))
    averages, _, scales = centre(third, fold3)
    lane = lax.broadcasted_iota(jnp.int32, (1, 256), 1)
    row = lax.broadcasted_iota(jnp.int32, (TILE, 256), 0)
    parts = [part for b in range(batch) for part in split(averages[b]) + split(scales[b])]
    parts.append(jnp.zeros((-len(parts) % TILE, third[0].shape[1]), F32))
    picked = jnp.dot(jnp.concatenate(parts, axis=0).astype(BF16), pick, preferred_element_type=F32)
    names = jnp.zeros((1, 256), F32)
    for k in range(owned):
        names = jnp.where(lane == NAMES + k, named[k].astype(F32), names)
    notes = jnp.zeros((TILE, 256), F32)
    for b in range(batch):
        note = names
        for k in range(2 * PARTS):
            at = 2 * PARTS * b + k
            note = jnp.where(lane // GROUPS == k, picked[at : at + 1], note)
        notes = jnp.where(row == step * batch + b, note, notes)
    body = sends[0].shape[0] - TILE
    for j in range(shares):
        q = me ^ j
        for b in range(batch):
            part = act[b, pl.ds(pl.multiple_of(q * share, share), share), :]
            part = jnp.dot(swap, part, preferred_element_type=F32).astype(BF16)
            sends[j][pl.ds(pl.multiple_of((step * batch + b) * share, share), share), :] = part

        @pl.when(step == 0)
        def _():
            sends[j][body : body + TILE, :] = notes.astype(BF16)

        @pl.when(step > 0)
        def _():
            held = sends[j][body : body + TILE, :].astype(F32)
            sends[j][body : body + TILE, :] = (held + notes).astype(BF16)


def encode(named, pixels, weights, shares):
    w1, g1, w2, g2, w3 = weights
    owned, frames, places, breadth = pixels.shape
    latent = frames // 2
    c1, c2, c3 = w1.shape[1], w2.shape[2], w3.shape[1]
    share = latent * places // shares
    tables, starts = stacked([
        spread_table(latent, 2 * GRID),
        swap_table(latent, places // shares),
        fold_table(c1, c1),
        fold_table(c2, c2),
        fold_table(c3, 256),
        pick_table(c3),
    ])
    operands = [w1, g1.reshape(1, c1), w2.reshape(3, 3 * w2.shape[1], c2), g2.reshape(1, c2), w3]
    operands.append(jnp.asarray(tables))
    body = owned * share + TILE
    flops = 2 * frames * places * breadth * c1 + 2 * latent * places * (27 * c1 * c2 + c2 * c3)
    return pl.pallas_call(
        functools.partial(encode_kernel, starts=starts, shares=shares, owned=owned),
        grid_spec=pltpu.PrefetchScalarGridSpec(
            num_scalar_prefetch=1,
            grid=(owned // BATCH,),
            in_specs=[pl.BlockSpec(memory_space=pltpu.HBM)] * (1 + len(operands)),
            out_specs=[pl.BlockSpec((body, c2), lambda i, s: (0, 0))] * shares,
            scratch_shapes=[pltpu.VMEM(o.shape, o.dtype) for o in operands]
            + [
                pltpu.VMEM((BATCH, frames, places, breadth), BF16),
                pltpu.VMEM((BATCH, (GRID + 2) * GRID * latent, 9 * c1), BF16),
                pltpu.VMEM((BATCH, places * latent, c2), BF16),
                pltpu.SemaphoreType.DMA((len(operands),)),
                pltpu.SemaphoreType.DMA((BATCH,)),
            ],
        ),
        out_shape=[jax.ShapeDtypeStruct((body, c2), BF16)] * shares,
        compiler_params=pltpu.CompilerParams(vmem_limit_bytes=44 * 1024 * 1024),
        cost_estimate=pl.CostEstimate(
            flops=owned * flops, bytes_accessed=owned * frames * places * breadth * 2, transcendentals=0
        ),
        name="encode",
    )(named, *[pltpu.with_memory_space_constraint(o, pltpu.HBM) for o in (pixels, *operands)])


def pack_kernel(ints, *rest, half, jobs, pick, owned, share):
    arrays = sum(len(job) for job in jobs)
    held, outs = rest[:arrays], rest[arrays:]
    me = lax.axis_index("patch").astype(jnp.int32)
    node = lax.axis_index("clip").astype(jnp.int32)
    owners = len(jobs[0])
    body = owned * share
    notes = jnp.concatenate([held[k][body : body + TILE, :] for k in range(owners)], axis=0)
    width = owners * TILE
    rows = lax.broadcasted_iota(jnp.int32, (TILE, width), 0)
    columns = lax.broadcasted_iota(jnp.int32, (TILE, width), 1)
    for s in range(half):
        sel = jnp.zeros((TILE, width), jnp.bool_)
        for j in range(owners):
            seen = jnp.int32(0)
            found = [jnp.int32(0)] * CAP
            for i in range(owned):
                mine = ints[j * owned + i] == (node ^ s)
                for r in range(CAP):
                    found[r] = jnp.where(mine & (seen == r), i, found[r])
                seen = seen + mine.astype(jnp.int32)
            for r in range(CAP):
                row = pick(me ^ jobs[0][j]) * CAP + r
                to = pl.ds(pl.multiple_of(row * share, share), share)
                at = pl.ds(pl.multiple_of(found[r] * share, share), share)
                sel = sel | ((rows == jnp.where(seen > r, row, -1)) & (columns == j * TILE + found[r]))
                for g in range(len(jobs)):
                    outs[g * half + s][to, :] = held[g * owners + j][at, :]
        sel = jnp.where(sel, 1.0, 0.0).astype(BF16)
        ready = jnp.dot(sel, notes, preferred_element_type=F32).astype(BF16)
        for g in range(len(jobs)):
            outs[g * half + s][owners * CAP * share :, :] = ready


def pack(half, held, jobs, pick, owned, share):
    owners, channels = len(jobs[0]), held[0].shape[1]
    names = [h[owned * share, NAMES : NAMES + owned] for h in held[:owners]]
    ints = jnp.concatenate(names).astype(jnp.int32)
    out_rows = owners * CAP * share + TILE
    count = len(jobs) * half
    outs = pl.pallas_call(
        functools.partial(pack_kernel, half=half, jobs=jobs, pick=pick, owned=owned, share=share),
        grid_spec=pltpu.PrefetchScalarGridSpec(
            num_scalar_prefetch=1,
            grid=(1,),
            in_specs=[pl.BlockSpec(h.shape, lambda i, s: (0, 0)) for h in held],
            out_specs=[pl.BlockSpec((out_rows, channels), lambda i, s: (0, 0))] * count,
        ),
        out_shape=[jax.ShapeDtypeStruct((out_rows, channels), BF16)] * count,
        compiler_params=pltpu.CompilerParams(vmem_limit_bytes=16 * 1024 * 1024),
        cost_estimate=pl.CostEstimate(flops=0, bytes_accessed=2 * count * out_rows * channels, transcendentals=0),
        name="pack",
    )(ints, *held)
    return [outs[g * half : (g + 1) * half] for g in range(len(jobs))]


def finish_kernel(places, w3, g3, place, *rest, count):
    taken, (out, ready, sems) = rest[:count], rest[-3:]
    c3 = w3.shape[1]
    _, lines, cores, _, cap, latent, share, _ = ready.shape
    rows = latent * share
    owners = [(line, core) for line in range(lines) for core in range(cores)]
    tail = len(owners) * cap * rows
    notes = jnp.concatenate([taken[i][tail : tail + TILE, :] for i in range(count)], axis=0)
    wide = jnp.dot(notes, place[...], preferred_element_type=F32)
    mean, gain = wide[:, :c3], wide[:, c3:] * g3[...]
    copies = []
    for i in range(count):
        for p, (line, core) in enumerate(owners):
            block = taken[i][p * cap * rows : (p + 1) * cap * rows, :]
            third = jnp.dot(block, w3[...], preferred_element_type=F32)
            for r in range(cap):
                at = i * TILE + p * cap + r
                token = (third[r * rows : (r + 1) * rows] - mean[at : at + 1]) * gain[at : at + 1]
                ready[i, line, core, 0, r] = token.reshape(latent, share, c3).astype(BF16)
        spot = out.at[
            pl.ds(places[3 * i] * lines, lines), pl.ds(places[3 * i + 1] * cores, cores), pl.ds(places[3 * i + 2], 1)
        ]
        copies.append(pltpu.make_async_copy(ready.at[i], spot, sems.at[i]))
        copies[i].start()
    for copy in copies:
        copy.wait()


def finish(pieces, block, w3, g3, shape, before=None):
    count = len(pieces)
    cap, latent, share, c3 = shape[3:]
    rows = latent * share
    c2 = w3.shape[0]
    arrays = [piece[3] for piece in pieces]
    places = jnp.stack([jnp.asarray(piece[k], jnp.int32) for piece in pieces for k in range(3)])
    place = jnp.asarray(place_table(c3).astype(ml_dtypes.bfloat16))
    operands = [w3, g3, place, *arrays]
    specs = [pl.BlockSpec(o.shape, lambda k, s: (0, 0)) for o in operands]
    aliases = {}
    if before is not None:
        specs.append(pl.BlockSpec(memory_space=pl.ANY))
        aliases = {1 + len(operands): 0}
        operands.append(before)
    blocks = count * block[0] * block[1] * cap
    return pl.pallas_call(
        functools.partial(finish_kernel, count=count),
        grid_spec=pltpu.PrefetchScalarGridSpec(
            num_scalar_prefetch=1,
            grid=(1,),
            in_specs=specs,
            out_specs=pl.BlockSpec(memory_space=pl.ANY),
            scratch_shapes=[
                pltpu.VMEM((count, *block, 1, cap, latent, share, c3), BF16),
                pltpu.SemaphoreType.DMA((count,)),
            ],
        ),
        out_shape=jax.ShapeDtypeStruct(shape, BF16),
        input_output_aliases=aliases,
        compiler_params=pltpu.CompilerParams(vmem_limit_bytes=24 * 1024 * 1024),
        cost_estimate=pl.CostEstimate(
            flops=2 * blocks * rows * c2 * c3, bytes_accessed=blocks * rows * (c2 + c3) * 2, transcendentals=0
        ),
        name="finish",
    )(places, *operands)


def on_device(pixels, destination, embed_weight, embed_gain, mixing_weight, mixing_gain, project_weight, project_gain):
    nodes, shares = lax.axis_size("clip"), lax.axis_size("patch")
    node = lax.axis_index("clip").astype(jnp.int32)
    half = nodes // 2
    owned, frames, places, _ = pixels.shape
    latent, c3 = frames // 2, project_weight.shape[1]
    share = latent * places // shares
    weights = (embed_weight, embed_gain, mixing_weight, mixing_gain, project_weight)
    named = destination.reshape(owned)

    me = lax.axis_index("patch").astype(jnp.int32)
    lines = shares // 2
    w3, g3 = project_weight, project_gain.reshape(1, c3)
    shape = (lines, 2, nodes, CAP, latent, places // shares, c3)

    def send(array, s, j):
        if s == 0 and j == 0:
            return array
        pairs = [(c * shares + p, (c ^ s) * shares + (p ^ j)) for c in range(nodes) for p in range(shares)]
        return lax.ppermute(array, ("clip", "patch"), pairs)

    sends = encode(named, pixels, weights, shares)
    held = [sends[0::2], [send(array, 0, 1) for array in sends[1::2]]]
    pairs = [[held[0][k], held[1][k]] for k in range(lines)]
    own = pack(half, [a for pair in pairs for a in pair], [[0, 1]] * lines, lambda p: p % 2, owned, share)
    def after(arrays, *earlier):
        return list(lax.optimization_barrier((*arrays, *earlier))[: len(arrays)])

    crossed = [send(held[0][k], half, 2 * k) for k in range(lines)]
    arrived = [[send(own[k][s], s, 2 * k) for s in range(half)] for k in range(lines)]
    pieces = [((me // 2) ^ k, 0, node ^ s, arrived[k][s]) for k in range(lines) for s in range(half)]
    beyond = after(held[1], crossed[0], *[a for line in own for a in line], arrived[1][half - 1])
    beyond = [send(beyond[k], half, 2 * k) for k in range(lines)]
    early, late = [], []
    for b, far in enumerate((crossed, beyond)):
        if b:
            far = after(far, *[a for line in arrived[1:] for a in line], *arrived[0])
        (other,) = pack(half, far, [[2 * k + b for k in range(lines)]], lambda p: p // 2, owned, share)
        arrivals = [(0, (me % 2) ^ b, node ^ half ^ s, send(other[s], s, 0)) for s in range(half)]
        early += arrivals if b == 0 else arrivals[:1]
        late = arrivals[1:]
    latents = finish(pieces, (1, 2), w3, g3, shape)
    latents = finish(early, (lines, 1), w3, g3, shape, latents)
    latents = finish(late, (lines, 1), w3, g3, shape, latents)
    return latents.reshape(shares * nodes * CAP, latent, places // shares, c3)


def solution(mesh):
    return jax.shard_map(
        on_device,
        mesh=mesh,
        in_specs=(
            P(("clip", "patch"), None, None, None),
            P(("clip", "patch"), None),
            P(),
            P(),
            P(),
            P(),
            P(),
            P(),
        ),
        out_specs=P("clip", None, "patch", None),
        check_vma=False,
    )
```

```python
import functools

import jax
import jax.numpy as jnp
import ml_dtypes
import numpy as np
from jax import lax
from jax.experimental import pallas as pl
from jax.experimental.pallas import tpu as pltpu
from jax.sharding import PartitionSpec as P

GRID = 8
GROUPS = 32
CAP = 2
TILE = 16
PARTS = 3
BATCH = 4
NAMES = 2 * PARTS * GROUPS
F32, BF16 = jnp.float32, jnp.bfloat16


def spread_table(latent, chunk):
    table = np.zeros((3, chunk, latent, 2 * latent, chunk), np.float32)
    places = np.arange(chunk)
    for tap in range(3):
        for step in range(latent):
            if 2 * step - 1 + tap >= 0:
                table[tap, places, step, 2 * step - 1 + tap, places] = 1
    return table.reshape(3 * chunk * latent, 2 * latent * chunk)


def swap_table(latent, share):
    table = np.zeros((latent, share, share, latent), np.float32)
    for step in range(latent):
        table[step, np.arange(share), np.arange(share), step] = 1
    return table.reshape(latent * share, latent * share)


def fold_table(channels, lanes):
    width = channels // GROUPS
    group = np.arange(lanes) // width
    return (group[:, None] == group[None, :]).astype(np.float32) / width


def pick_table(channels):
    table = np.zeros((channels, 256), np.float32)
    lanes = np.arange(NAMES)
    table[lanes % GROUPS * (channels // GROUPS), lanes] = 1
    return table


def place_table(channels):
    table = np.zeros((256, 2, channels), np.float32)
    lanes = np.arange(NAMES)
    of_group = lanes[:, None] % GROUPS == np.arange(channels)[None, :] // (channels // GROUPS)
    for which in range(2):
        mine = lanes // (PARTS * GROUPS) == which
        table[:NAMES, which] = of_group & mine[:, None]
    return table.reshape(256, 2 * channels)


def stacked(tables):
    rows = [np.pad(t, ((0, 0), (0, 256 - t.shape[1]))) for t in tables]
    starts = np.cumsum([0] + [r.shape[0] for r in rows])
    return np.concatenate(rows).astype(ml_dtypes.bfloat16), [int(s) for s in starts]


def split(row):
    parts = []
    for _ in range(PARTS):
        head = row.astype(BF16)
        parts.append(head.astype(F32))
        row = row - head.astype(F32)
    return parts


def fold(rows, table):
    lanes = table.shape[0]
    halves = rows[0].shape[1] // lanes
    stack = []
    for row in rows:
        parts = split(row)
        stack += [part[:, h * lanes : (h + 1) * lanes] for h in range(halves) for part in parts]
    spare = -len(stack) % TILE
    if spare:
        stack.append(jnp.zeros((spare, lanes), F32))
    out = jnp.dot(jnp.concatenate(stack, axis=0).astype(BF16), table, preferred_element_type=F32)
    sums = []
    for k in range(0, len(rows) * halves, halves):
        at = [PARTS * (k + h) for h in range(halves)]
        sums.append(jnp.concatenate([jnp.sum(out[i : i + PARTS], axis=0, keepdims=True) for i in at], axis=1))
    return sums


def centre(values, table):
    share = 1.0 / values[0].shape[0]
    averages = fold([jnp.sum(v, axis=0, keepdims=True) * share for v in values], table)
    centred = [v - average for v, average in zip(values, averages)]
    powers = fold([jnp.sum(v * v, axis=0, keepdims=True) * share for v in centred], table)
    return averages, centred, [lax.rsqrt(power + 1e-05) for power in powers]


def silu(v):
    half = 0.5 * v
    return half + half * jnp.tanh(half)


def encode_kernel(named, x, *rest, starts, shares, owned):
    given, rest = rest[:6], rest[6:]
    sends, rest = rest[:shares], rest[shares:]
    (w1, g1, w2, g2, w3, tables), (tubes, wide, act, sems, tube_sems) = rest[:6], rest[6:]
    me = lax.axis_index("patch").astype(jnp.int32)
    copies = [pltpu.make_async_copy(a, b, sems.at[i]) for i, (a, b) in enumerate(zip(given, rest[:6]))]
    step = pl.program_id(0)

    def arrive(*which):
        @pl.when(step == 0)
        def _():
            for i in which:
                copies[i].wait()

    batch, frames, places, breadth = tubes.shape
    loads = [pltpu.make_async_copy(x.at[step * batch + b], tubes.at[b], tube_sems.at[b]) for b in range(batch)]
    latent = frames // 2
    c1, c2 = w1.shape[1], w2.shape[2]
    line = GRID * latent
    share = places * latent // shares
    chunk = 2 * GRID
    rows = places * latent

    @pl.when(step == 0)
    def _():
        copies[0].start()

    loads[0].start()

    @pl.when(step == 0)
    def _():
        copies[5].start()
        copies[1].start()

    for load in loads[1:]:
        load.start()

    @pl.when(step == 0)
    def _():
        for i in (2, 3, 4):
            copies[i].start()
        for b in range(batch):
            wide[b, 0:line, :] = jnp.zeros((line, wide.shape[2]), BF16)
            wide[b, (GRID + 1) * line :, :] = jnp.zeros((line, wide.shape[2]), BF16)

    arrive(0, 5, 1)
    spread = tables[starts[0] : starts[1]]
    swap = tables[starts[1] : starts[2], 0:share]
    fold1 = tables[starts[2] : starts[3], 0:c1]
    fold2 = tables[starts[3] : starts[4], 0:c2]
    fold3 = tables[starts[4] : starts[5]]
    pick = tables[starts[5] : starts[6]]
    first = []
    for b in range(batch):
        loads[b].wait()
        first.append(jnp.dot(tubes[b].reshape(frames * places, breadth), w1[...], preferred_element_type=F32))
    _, centred, scales = centre(first, fold1)
    for b in range(batch):
        act1 = silu(centred[b] * (scales[b] * g1[...])).astype(BF16).reshape(frames, places, c1)
        for q in range(places // chunk):
            block = act1[:, q * chunk : (q + 1) * chunk].reshape(frames * chunk, c1)
            taps = jnp.dot(spread, block, preferred_element_type=F32)
            taps = taps.reshape(3, chunk // GRID, GRID, latent, c1)
            edge = jnp.zeros((chunk // GRID, 1, latent, c1), F32)
            at = line + q * chunk * latent
            for a in range(3):
                for j in range(3):
                    tap = taps[a]
                    if j == 0:
                        tap = jnp.concatenate([edge, tap[:, : GRID - 1]], axis=1)
                    if j == 2:
                        tap = jnp.concatenate([tap[:, 1:], edge], axis=1)
                    tap = tap.reshape(chunk * latent, c1).astype(BF16)
                    wide[b, at : at + chunk * latent, (3 * j + a) * c1 : (3 * j + a + 1) * c1] = tap
    arrive(2, 3, 4)
    second = []
    for b in range(batch):
        total = jnp.dot(wide[b, 0:rows], w2[0], preferred_element_type=F32)
        for i in (1, 2):
            total += jnp.dot(wide[b, i * line : i * line + rows], w2[i], preferred_element_type=F32)
        second.append(total)
    _, centred, scales = centre(second, fold2)
    third = []
    for b in range(batch):
        act2 = silu(centred[b] * (scales[b] * g2[...])).astype(BF16)
        act[b] = act2
        third.append(jnp.dot(act2, w3[...], preferred_element_type=F32))
    averages, _, scales = centre(third, fold3)
    lane = lax.broadcasted_iota(jnp.int32, (1, 256), 1)
    row = lax.broadcasted_iota(jnp.int32, (TILE, 256), 0)
    parts = [part for b in range(batch) for part in split(averages[b]) + split(scales[b])]
    parts.append(jnp.zeros((-len(parts) % TILE, third[0].shape[1]), F32))
    picked = jnp.dot(jnp.concatenate(parts, axis=0).astype(BF16), pick, preferred_element_type=F32)
    names = jnp.zeros((1, 256), F32)
    for k in range(owned):
        names = jnp.where(lane == NAMES + k, named[k].astype(F32), names)
    notes = jnp.zeros((TILE, 256), F32)
    for b in range(batch):
        note = names
        for k in range(2 * PARTS):
            at = 2 * PARTS * b + k
            note = jnp.where(lane // GROUPS == k, picked[at : at + 1], note)
        notes = jnp.where(row == step * batch + b, note, notes)
    body = sends[0].shape[0] - TILE
    for j in range(shares):
        q = me ^ j
        for b in range(batch):
            part = act[b, pl.ds(pl.multiple_of(q * share, share), share), :]
            part = jnp.dot(swap, part, preferred_element_type=F32).astype(BF16)
            sends[j][pl.ds(pl.multiple_of((step * batch + b) * share, share), share), :] = part

        @pl.when(step == 0)
        def _():
            sends[j][body : body + TILE, :] = notes.astype(BF16)

        @pl.when(step > 0)
        def _():
            held = sends[j][body : body + TILE, :].astype(F32)
            sends[j][body : body + TILE, :] = (held + notes).astype(BF16)


def encode(named, pixels, weights, shares):
    w1, g1, w2, g2, w3 = weights
    owned, frames, places, breadth = pixels.shape
    latent = frames // 2
    c1, c2, c3 = w1.shape[1], w2.shape[2], w3.shape[1]
    share = latent * places // shares
    tables, starts = stacked([
        spread_table(latent, 2 * GRID),
        swap_table(latent, places // shares),
        fold_table(c1, c1),
        fold_table(c2, c2),
        fold_table(c3, 256),
        pick_table(c3),
    ])
    operands = [w1, g1.reshape(1, c1), w2.reshape(3, 3 * w2.shape[1], c2), g2.reshape(1, c2), w3]
    operands.append(jnp.asarray(tables))
    body = owned * share + TILE
    flops = 2 * frames * places * breadth * c1 + 2 * latent * places * (27 * c1 * c2 + c2 * c3)
    return pl.pallas_call(
        functools.partial(encode_kernel, starts=starts, shares=shares, owned=owned),
        grid_spec=pltpu.PrefetchScalarGridSpec(
            num_scalar_prefetch=1,
            grid=(owned // BATCH,),
            in_specs=[pl.BlockSpec(memory_space=pltpu.HBM)] * (1 + len(operands)),
            out_specs=[pl.BlockSpec((body, c2), lambda i, s: (0, 0))] * shares,
            scratch_shapes=[pltpu.VMEM(o.shape, o.dtype) for o in operands]
            + [
                pltpu.VMEM((BATCH, frames, places, breadth), BF16),
                pltpu.VMEM((BATCH, (GRID + 2) * GRID * latent, 9 * c1), BF16),
                pltpu.VMEM((BATCH, places * latent, c2), BF16),
                pltpu.SemaphoreType.DMA((len(operands),)),
                pltpu.SemaphoreType.DMA((BATCH,)),
            ],
        ),
        out_shape=[jax.ShapeDtypeStruct((body, c2), BF16)] * shares,
        compiler_params=pltpu.CompilerParams(vmem_limit_bytes=44 * 1024 * 1024),
        cost_estimate=pl.CostEstimate(
            flops=owned * flops, bytes_accessed=owned * frames * places * breadth * 2, transcendentals=0
        ),
        name="encode",
    )(*[pltpu.with_memory_space_constraint(o, pltpu.HBM) for o in (named, pixels, *operands)])


def pack_kernel(ints, *rest, half, jobs, pick, owned, share):
    arrays = sum(len(job) for job in jobs)
    held, outs = rest[:arrays], rest[arrays:]
    me = lax.axis_index("patch").astype(jnp.int32)
    node = lax.axis_index("clip").astype(jnp.int32)
    owners = len(jobs[0])
    body = owned * share
    notes = jnp.concatenate([held[k][body : body + TILE, :] for k in range(owners)], axis=0)
    width = owners * TILE
    rows = lax.broadcasted_iota(jnp.int32, (TILE, width), 0)
    columns = lax.broadcasted_iota(jnp.int32, (TILE, width), 1)
    for s in range(half):
        sel = jnp.zeros((TILE, width), jnp.bool_)
        for j in range(owners):
            seen = jnp.int32(0)
            found = [jnp.int32(0)] * CAP
            for i in range(owned):
                mine = ints[j * owned + i] == (node ^ s)
                for r in range(CAP):
                    found[r] = jnp.where(mine & (seen == r), i, found[r])
                seen = seen + mine.astype(jnp.int32)
            for r in range(CAP):
                row = pick(me ^ jobs[0][j]) * CAP + r
                to = pl.ds(pl.multiple_of(row * share, share), share)
                at = pl.ds(pl.multiple_of(found[r] * share, share), share)
                sel = sel | ((rows == jnp.where(seen > r, row, -1)) & (columns == j * TILE + found[r]))
                for g in range(len(jobs)):
                    outs[g * half + s][to, :] = held[g * owners + j][at, :]
        sel = jnp.where(sel, 1.0, 0.0).astype(BF16)
        ready = jnp.dot(sel, notes, preferred_element_type=F32).astype(BF16)
        for g in range(len(jobs)):
            outs[g * half + s][owners * CAP * share :, :] = ready


def pack(half, held, jobs, pick, owned, share):
    owners, channels = len(jobs[0]), held[0].shape[1]
    names = [h[owned * share, NAMES : NAMES + owned] for h in held[:owners]]
    ints = jnp.concatenate(names).astype(jnp.int32)
    out_rows = owners * CAP * share + TILE
    count = len(jobs) * half
    outs = pl.pallas_call(
        functools.partial(pack_kernel, half=half, jobs=jobs, pick=pick, owned=owned, share=share),
        grid_spec=pltpu.PrefetchScalarGridSpec(
            num_scalar_prefetch=1,
            grid=(1,),
            in_specs=[pl.BlockSpec(h.shape, lambda i, s: (0, 0)) for h in held],
            out_specs=[pl.BlockSpec((out_rows, channels), lambda i, s: (0, 0))] * count,
        ),
        out_shape=[jax.ShapeDtypeStruct((out_rows, channels), BF16)] * count,
        compiler_params=pltpu.CompilerParams(vmem_limit_bytes=16 * 1024 * 1024),
        cost_estimate=pl.CostEstimate(flops=0, bytes_accessed=2 * count * out_rows * channels, transcendentals=0),
        name="pack",
    )(ints, *held)
    return [outs[g * half : (g + 1) * half] for g in range(len(jobs))]


def finish_kernel(places, w3, g3, place, *rest, count):
    taken, (out, ready, sems) = rest[:count], rest[-3:]
    c3 = w3.shape[1]
    _, lines, cores, _, cap, latent, share, _ = ready.shape
    rows = latent * share
    owners = [(line, core) for line in range(lines) for core in range(cores)]
    tail = len(owners) * cap * rows
    notes = jnp.concatenate([taken[i][tail : tail + TILE, :] for i in range(count)], axis=0)
    wide = jnp.dot(notes, place[...], preferred_element_type=F32)
    mean, gain = wide[:, :c3], wide[:, c3:] * g3[...]
    copies = []
    for i in range(count):
        for p, (line, core) in enumerate(owners):
            block = taken[i][p * cap * rows : (p + 1) * cap * rows, :]
            third = jnp.dot(block, w3[...], preferred_element_type=F32)
            for r in range(cap):
                at = i * TILE + p * cap + r
                token = (third[r * rows : (r + 1) * rows] - mean[at : at + 1]) * gain[at : at + 1]
                ready[i, line, core, 0, r] = token.reshape(latent, share, c3).astype(BF16)
        spot = out.at[
            pl.ds(places[3 * i] * lines, lines), pl.ds(places[3 * i + 1] * cores, cores), pl.ds(places[3 * i + 2], 1)
        ]
        copies.append(pltpu.make_async_copy(ready.at[i], spot, sems.at[i]))
        copies[i].start()
    for copy in copies:
        copy.wait()


def finish(pieces, block, w3, g3, shape, before=None):
    count = len(pieces)
    cap, latent, share, c3 = shape[3:]
    rows = latent * share
    c2 = w3.shape[0]
    arrays = [piece[3] for piece in pieces]
    places = jnp.stack([jnp.asarray(piece[k], jnp.int32) for piece in pieces for k in range(3)])
    place = jnp.asarray(place_table(c3).astype(ml_dtypes.bfloat16))
    operands = [w3, g3, place, *arrays]
    specs = [pl.BlockSpec(o.shape, lambda k, s: (0, 0)) for o in operands]
    aliases = {}
    if before is not None:
        specs.append(pl.BlockSpec(memory_space=pl.ANY))
        aliases = {1 + len(operands): 0}
        operands.append(before)
    blocks = count * block[0] * block[1] * cap
    return pl.pallas_call(
        functools.partial(finish_kernel, count=count),
        grid_spec=pltpu.PrefetchScalarGridSpec(
            num_scalar_prefetch=1,
            grid=(1,),
            in_specs=specs,
            out_specs=pl.BlockSpec(memory_space=pl.ANY),
            scratch_shapes=[
                pltpu.VMEM((count, *block, 1, cap, latent, share, c3), BF16),
                pltpu.SemaphoreType.DMA((count,)),
            ],
        ),
        out_shape=jax.ShapeDtypeStruct(shape, BF16),
        input_output_aliases=aliases,
        compiler_params=pltpu.CompilerParams(vmem_limit_bytes=24 * 1024 * 1024),
        cost_estimate=pl.CostEstimate(
            flops=2 * blocks * rows * c2 * c3, bytes_accessed=blocks * rows * (c2 + c3) * 2, transcendentals=0
        ),
        name="finish",
    )(places, *operands)


def on_device(pixels, destination, embed_weight, embed_gain, mixing_weight, mixing_gain, project_weight, project_gain):
    nodes, shares = lax.axis_size("clip"), lax.axis_size("patch")
    node = lax.axis_index("clip").astype(jnp.int32)
    half = nodes // 2
    owned, frames, places, _ = pixels.shape
    latent, c3 = frames // 2, project_weight.shape[1]
    share = latent * places // shares
    weights = (embed_weight, embed_gain, mixing_weight, mixing_gain, project_weight)
    named = destination.reshape(owned)

    me = lax.axis_index("patch").astype(jnp.int32)
    lines = shares // 2
    w3, g3 = project_weight, project_gain.reshape(1, c3)
    shape = (lines, 2, nodes, CAP, latent, places // shares, c3)

    def send(array, s, j):
        if s == 0 and j == 0:
            return array
        pairs = [(c * shares + p, (c ^ s) * shares + (p ^ j)) for c in range(nodes) for p in range(shares)]
        return lax.ppermute(array, ("clip", "patch"), pairs)

    sends = encode(named, pixels, weights, shares)
    held = [sends[0::2], [send(array, 0, 1) for array in sends[1::2]]]
    pairs = [[held[0][k], held[1][k]] for k in range(lines)]
    own = pack(half, [a for pair in pairs for a in pair], [[0, 1]] * lines, lambda p: p % 2, owned, share)
    def after(arrays, *earlier):
        return list(lax.optimization_barrier((*arrays, *earlier))[: len(arrays)])

    crossed = [send(held[0][k], half, 2 * k) for k in range(lines)]
    arrived = [[send(own[k][s], s, 2 * k) for s in range(half)] for k in range(lines)]
    pieces = [((me // 2) ^ k, 0, node ^ s, arrived[k][s]) for k in range(lines) for s in range(half)]
    beyond = after(held[1], crossed[0], *[a for line in own for a in line], arrived[1][half - 1])
    beyond = [send(beyond[k], half, 2 * k) for k in range(lines)]
    early, late = [], []
    for b, far in enumerate((crossed, beyond)):
        if b:
            far = after(far, *[a for line in arrived[1:] for a in line], *arrived[0])
        (other,) = pack(half, far, [[2 * k + b for k in range(lines)]], lambda p: p // 2, owned, share)
        arrivals = [(0, (me % 2) ^ b, node ^ half ^ s, send(other[s], s, 0)) for s in range(half)]
        early += arrivals if b == 0 else arrivals[:1]
        late = arrivals[1:]
    latents = finish(pieces, (1, 2), w3, g3, shape)
    latents = finish(early, (lines, 1), w3, g3, shape, latents)
    latents = finish(late, (lines, 1), w3, g3, shape, latents)
    return latents.reshape(shares * nodes * CAP, latent, places // shares, c3)


def solution(mesh):
    return jax.shard_map(
        on_device,
        mesh=mesh,
        in_specs=(
            P(("clip", "patch"), None, None, None),
            P(("clip", "patch"), None),
            P(),
            P(),
            P(),
            P(),
            P(),
            P(),
        ),
        out_specs=P("clip", None, "patch", None),
        check_vma=False,
    )
```
